32 devices in a mesh: fsdp: 2 (over core), context: 8 (over z, x), tensor: 2 (over y).
Axes of the slice: x: 2, y: 2, z: 4, core: 2. Of those that a mesh axis runs over, the one named last changes fastest.
Arguments:
- tokens: bfloat16 [8192, 1024], P(('fsdp', 'context')), may hold values from -6 to 6
- doc_blocks: int32 [2, 3], P('fsdp'), may hold values from 8 to 16, as said below
- pad_tokens: int32 [2, 3], P('fsdp'), may hold values from 0 to 127
- w_qkv: bfloat16 [1024, 3, 1024], P(('fsdp', 'context'), None, 'tensor'), may hold values from -0.25 to 0.25
- bias_query: float32 [1024], P('tensor'), may hold values from -3 to 3
- bias_value: float32 [1024], P('tensor'), may hold values from -3 to 3
- w_attn_out: bfloat16 [1024, 1024], P('tensor', ('fsdp', 'context')), may hold values from -1 to 1
- bias_attn_out: float32 [1024], replicated, may hold values from -3 to 3
- gain_one: float32 [1024], replicated, may hold values from 0.5 to 1.5
- shift_one: float32 [1024], replicated, may hold values from -3 to 3
- w_up: bfloat16 [1024, 4096], P(('fsdp', 'context'), 'tensor'), may hold values from -0.1875 to 0.1875
- bias_up: float32 [4096], P('tensor'), may hold values from -3 to 3
- w_down: bfloat16 [4096, 1024], P('tensor', ('fsdp', 'context')), may hold values from -0.125 to 0.125
- bias_down: float32 [1024], replicated, may hold values from -3 to 3
- gain_two: float32 [1024], replicated, may hold values from 0.5 to 1.5
- shift_two: float32 [1024], replicated, may hold values from -3 to 3
- cotangent: bfloat16 [8192, 1024], P(('fsdp', 'context')), may hold values from -6 to 6
Outputs:
- output: bfloat16 [8192, 1024], P(('fsdp', 'context'))
- grad_tokens: float32 [8192, 1024], P(('fsdp', 'context'))
- grad_w_qkv: float32 [1024, 3, 1024], P(('fsdp', 'context'), None, 'tensor')
- grad_bias_query: float32 [1024], P('tensor')
- grad_bias_value: float32 [1024], P('tensor')
- grad_w_attn_out: float32 [1024, 1024], P('tensor', ('fsdp', 'context'))
- grad_bias_attn_out: float32 [1024], replicated
- grad_gain_one: float32 [1024], replicated
- grad_shift_one: float32 [1024], replicated
- grad_w_up: float32 [1024, 4096], P(('fsdp', 'context'), 'tensor')
- grad_bias_up: float32 [4096], P('tensor')
- grad_w_down: float32 [4096, 1024], P('tensor', ('fsdp', 'context'))
- grad_bias_down: float32 [1024], replicated
- grad_gain_two: float32 [1024], replicated
- grad_shift_two: float32 [1024], replicated
The draws below stay inside these ranges and needn't reach their ends.
Inputs may be any that keep to these rules, and one draw needn't show every extreme that they name: `doc_blocks`: each row sums to 32; its largest entry is exactly 16.
All inputs are finite; a program needn't handle non-finite values.
Results may differ from the reference program's by a relative error of at most 0.028.
Values may be sent and summed in bfloat16 or wider, within the bound.
A program may use at most 192 MiB of HBM per device.

```python
import jax
import jax.numpy as jnp
from jax import lax

D = 1024
HEADS = 16
HEAD = 64
FF = 4096
TOK_DEV = 512
BLK = 128
MAXB = 16
GROUP = 4096
TOKENS = 8192
NBLK = 32
NDOC = 3
QB = 512
N_FSDP = 2
N_CONTEXT = 8


def draw_doc_blocks(key, part):
    key = jax.random.fold_in(key, 7)
    least = MAXB // 2
    others = NDOC - 1
    spare = NBLK - least * NDOC - least

    def one_row(row_key):
        order_key, full_key = jax.random.split(row_key)
        order = jax.random.permutation(order_key, others * least)
        taken = (jnp.arange(others * least, dtype=jnp.int32) < spare).astype(jnp.int32)
        owner = order // least
        extra = jnp.sum((owner[:, None] == jnp.arange(others, dtype=jnp.int32)[None, :]).astype(jnp.int32) * taken[:, None], axis=0)
        rest = least + extra
        full_at = jax.random.randint(full_key, (), 0, NDOC)
        index = jnp.arange(NDOC, dtype=jnp.int32)
        pick = jnp.clip(index - (index > full_at).astype(jnp.int32), 0, others - 1)
        return jnp.where(index == full_at, MAXB, rest[pick]).astype(jnp.int32)
    return jax.vmap(one_row)(jax.random.split(key, N_FSDP))


def touch_ends(values, rng, low, top_value):
    place = [jax.random.randint(jax.random.fold_in(rng, axis), (), 0, length) for axis, length in enumerate(values.shape)]
    longest = values.shape.index(max(values.shape))
    beside = place[:longest] + [(place[longest] + 1) % values.shape[longest]] + place[longest + 1:]
    return values.at[tuple(place)].set(low).at[tuple(beside)].set(top_value)


def block_scale(rng, shape, cuts, smallest, high):
    def one(position, blocks):
        heights = jax.random.uniform(jax.random.fold_in(jax.random.fold_in(rng, 6), position), (blocks,), jnp.float32, smallest / len(cuts), high / len(cuts))
        return jnp.repeat(jnp.exp(heights), shape[position] // blocks).reshape((-1,) + (1,) * (len(shape) - position - 1))

    gain = one(*cuts[0])
    for cut in cuts[1:]:
        gain = gain * one(*cut)
    return gain


def normal_values(stream_key, shape, spread, reach, cuts=(), held_as=jnp.bfloat16):
    entries = spread * jax.random.normal(stream_key, shape, jnp.float32)
    if cuts:
        entries = entries * block_scale(stream_key, shape, cuts, -0.22, 0.18)
    return jnp.clip(entries, -reach, reach).astype(held_as)


def setup_inputs(seed: int = 0) -> dict:
    key_of = jax.random.split(jax.random.key(seed), 18)
    tokens = normal_values(key_of[0], (TOKENS, D), 1.0, 6.0, ((0, 16),))
    doc_blocks = draw_doc_blocks(jax.random.fold_in(key_of[17], 71), 0)
    pad_tokens = touch_ends(jax.random.randint(key_of[2], (N_FSDP, NDOC), 0, BLK), jax.random.fold_in(key_of[2], 1), 0, BLK - 1).astype(jnp.int32)
    w_qkv = normal_values(key_of[3], (D, 3, D), (D // 2) ** -0.5, 0.25, ((0, 16), (2, 2)))
    bias_query = normal_values(key_of[4], (D,), 0.5, 3.0, ((0, 2),), jnp.float32)
    bias_value = normal_values(key_of[5], (D,), 0.5, 3.0, ((0, 2),), jnp.float32)
    w_attn_out = normal_values(key_of[6], (D, D), (D // 32) ** -0.5, 1.0, ((0, 2), (1, 16)))
    bias_attn_out = normal_values(key_of[7], (D,), 0.5, 3.0, (), jnp.float32)
    gain_one = jnp.clip(1.0 + 0.1 * jax.random.normal(key_of[8], (D,), jnp.float32), 0.5, 1.5)
    shift_one = normal_values(key_of[9], (D,), 0.5, 3.0, (), jnp.float32)
    w_up = normal_values(key_of[10], (D, FF), D ** -0.5, 0.1875, ((0, 16), (1, 2)))
    bias_up = normal_values(key_of[11], (FF,), 0.5, 3.0, ((0, 2),), jnp.float32)
    w_down = normal_values(key_of[12], (FF, D), (FF // 2) ** -0.5, 0.125, ((0, 2), (1, 16)))
    bias_down = normal_values(key_of[13], (D,), 0.5, 3.0, (), jnp.float32)
    gain_two = jnp.clip(1.0 + 0.1 * jax.random.normal(key_of[14], (D,), jnp.float32), 0.5, 1.5)
    shift_two = normal_values(key_of[15], (D,), 0.5, 3.0, (), jnp.float32)
    cotangent = normal_values(key_of[16], (TOKENS, D), 1.0, 6.0, ((0, 16),))
    return dict(tokens=tokens, doc_blocks=doc_blocks, pad_tokens=pad_tokens, w_qkv=w_qkv, bias_query=bias_query, bias_value=bias_value, w_attn_out=w_attn_out, bias_attn_out=bias_attn_out, gain_one=gain_one, shift_one=shift_one, w_up=w_up, bias_up=bias_up, w_down=w_down, bias_down=bias_down, gain_two=gain_two, shift_two=shift_two, cotangent=cotangent)


@jax.custom_vjp
def low(v):
    return lax.optimization_barrier(v.astype(jnp.bfloat16)).astype(jnp.float32)

@jax.custom_vjp
def low_back(v):
    return v

def low_keep(v):
    return (low(v), None)

def low_pass(kept, grad):
    return (grad,)

def back_keep(v):
    return (v, None)

def back_low(kept, grad):
    return (low(grad),)
low.defvjp(low_keep, low_pass)
low_back.defvjp(back_keep, back_low)
EPSILON = 1e-05
MASKED = -1e+30
HIGHEST = lax.Precision.HIGHEST

def block_place(stored, contexts):
    local_row = stored % TOK_DEV
    owner = stored // TOK_DEV
    return (local_row // BLK * contexts + owner) * BLK + local_row % BLK

def doc_of(doc_row, pad_row, positions):
    doc_ends = (jnp.cumsum(doc_row) * BLK).astype(jnp.int32)
    doc_index = lax.optimization_barrier(jnp.sum((positions[:, None] >= doc_ends[None, :]).astype(jnp.int32), axis=1)).astype(jnp.int32)
    chosen = doc_index[:, None] == jnp.arange(doc_ends.shape[0], dtype=jnp.int32)[None, :]
    live_end = lax.optimization_barrier(jnp.sum(jnp.where(chosen, doc_ends - pad_row, 0), axis=1)).astype(jnp.int32)
    return (doc_index, positions < live_end)

def layer_norm(hidden, gain_vec, bias_add):
    row_mean = lax.optimization_barrier(jnp.mean(hidden, axis=-1, keepdims=True))
    centred = hidden - row_mean
    factor = lax.rsqrt(lax.optimization_barrier(jnp.mean(centred * centred, axis=-1, keepdims=True)) + EPSILON)
    return centred * factor * gain_vec + bias_add

def one_block(block_index, query_all, key_padded, value_padded, doc_all, doc_padded, live_padded):
    per_group = GROUP // QB
    window = QB + 2 * (MAXB - 1) * BLK
    group_index = block_index // per_group
    begin = block_index % per_group * QB
    query_block = lax.dynamic_slice_in_dim(query_all[group_index], begin, QB, 0)
    key_block = lax.dynamic_slice_in_dim(key_padded[group_index], begin, window, 0)
    value_block = lax.dynamic_slice_in_dim(value_padded[group_index], begin, window, 0)
    query_doc = lax.dynamic_slice_in_dim(doc_all[group_index], begin, QB, 0)
    key_doc = lax.dynamic_slice_in_dim(doc_padded[group_index], begin, window, 0)
    key_live = lax.dynamic_slice_in_dim(live_padded[group_index], begin, window, 0)
    scores = jnp.einsum('qhd,khd->hqk', query_block, key_block, precision=HIGHEST) * HEAD ** (-0.5)
    scores = low_back(scores)
    allowed = ((query_doc[:, None] == key_doc[None, :]) & key_live[None, :])[None]
    scores = jnp.where(allowed, scores, MASKED)
    row_top = lax.optimization_barrier(jnp.max(scores, axis=2, keepdims=True))
    expo = jnp.where(allowed, jnp.exp(scores - row_top), 0.0)
    prob_low = low(expo / lax.optimization_barrier(jnp.sum(expo, axis=2, keepdims=True)))
    return jnp.einsum('hqk,khd->qhd', prob_low, value_block, precision=HIGHEST)

def attention(query_all, key_all, value_all, doc_all, live_all):
    margin = (MAXB - 1) * BLK
    widths = ((0, 0), (margin, margin), (0, 0), (0, 0))
    key_padded = jnp.pad(key_all, widths)
    value_padded = jnp.pad(value_all, widths)
    doc_padded = jnp.pad(doc_all, ((0, 0), (margin, margin)), constant_values=-1)
    live_padded = jnp.pad(live_all, ((0, 0), (margin, margin)))
    blocked = jax.checkpoint(one_block)
    count = N_FSDP * (GROUP // QB)
    result = lax.map(lambda block_index: blocked(block_index, query_all, key_padded, value_padded, doc_all, doc_padded, live_padded), jnp.arange(count, dtype=jnp.int32))
    return result.reshape(N_FSDP, GROUP, HEADS * HEAD)

def forward(inputs, w_qkv, bias_query, bias_value, w_attn_out, bias_attn_out, gain_one, shift_one, w_up, bias_up, w_down, bias_down, gain_two, shift_two, doc_all, live_all):
    bias_three = jnp.stack([bias_query, jnp.zeros_like(bias_query), bias_value])
    qkv = jnp.einsum('gtd,dce->gtce', inputs, w_qkv, precision=HIGHEST) + bias_three
    qkv = low(low_back(qkv))
    head_shape = (N_FSDP, GROUP, HEADS, HEAD)
    attended = attention(qkv[:, :, 0].reshape(head_shape), qkv[:, :, 1].reshape(head_shape), qkv[:, :, 2].reshape(head_shape), doc_all, live_all)
    attended = low(low_back(attended))
    branch = low_back(jnp.einsum('gte,ed->gtd', attended, w_attn_out, precision=HIGHEST) + bias_attn_out)
    first = layer_norm(inputs + branch, gain_one, shift_one)
    pre = low_back(jnp.einsum('gtd,df->gtf', low(first), w_up, precision=HIGHEST) + bias_up)
    act = low(jax.nn.gelu(pre, approximate=False))
    feed = low_back(jnp.einsum('gtf,fd->gtd', act, w_down, precision=HIGHEST) + bias_down)
    return layer_norm(first + feed, gain_two, shift_two)

def reference(tokens, doc_blocks, pad_tokens, w_qkv, bias_query, bias_value, w_attn_out, bias_attn_out, gain_one, shift_one, w_up, bias_up, w_down, bias_down, gain_two, shift_two, cotangent):
    group_rows = jnp.arange(GROUP, dtype=jnp.int32)
    positions = block_place(group_rows, N_CONTEXT).astype(jnp.int32)
    anchor = jnp.zeros((GROUP,), jnp.int32).at[positions].set(group_rows)
    inputs = tokens.astype(jnp.float32).reshape(N_FSDP, GROUP, D)[:, anchor]
    seed_grad = cotangent.astype(jnp.float32).reshape(N_FSDP, GROUP, D)[:, anchor]
    doc_all, live_all = jax.vmap(lambda doc_row, pad_row: doc_of(doc_row, pad_row, group_rows))(doc_blocks, pad_tokens)
    params = (w_qkv.astype(jnp.float32), bias_query, bias_value, w_attn_out.astype(jnp.float32), bias_attn_out, gain_one, shift_one, w_up.astype(jnp.float32), bias_up, w_down.astype(jnp.float32), bias_down, gain_two, shift_two)
    result, pull = jax.vjp(lambda *values: forward(*values, doc_all, live_all), inputs, *params)
    grads = pull(seed_grad)
    output = result[:, positions].reshape(TOKENS, D).astype(jnp.bfloat16)
    grad_tokens = grads[0][:, positions].reshape(TOKENS, D)
    return (output, grad_tokens, grads[1], grads[2], grads[3], grads[4], grads[5], grads[6], grads[7], grads[8], grads[9], grads[10], grads[11], grads[12], grads[13])
```

```python
import functools

import jax
import jax.numpy as jnp
from jax import lax
from jax.experimental import pallas as pl
from jax.experimental.pallas import tpu as pltpu
from jax.sharding import PartitionSpec as P

HEAD = 64
TOK_DEV = 512
BLK = 128
MAXB = 16
QB = 512


EPSILON = 1e-05
MASKED = -1e30


def block_place(stored, contexts):
    local_row = stored % TOK_DEV
    owner = stored // TOK_DEV
    return (local_row // BLK * contexts + owner) * BLK + local_row % BLK


def doc_of(doc_row, pad_row, positions):
    doc_ends = jnp.cumsum(doc_row) * BLK
    doc_index = jnp.sum((positions[:, None] >= doc_ends[None, :]).astype(jnp.int32), axis=1)
    chosen = doc_index[:, None] == jnp.arange(doc_ends.shape[0], dtype=jnp.int32)[None, :]
    live_end = jnp.sum(jnp.where(chosen, doc_ends - pad_row, 0), axis=1)
    return (doc_index, positions < live_end)


def layer_norm(hidden, gain_vec, bias_add):
    row_mean = jnp.mean(hidden, axis=-1, keepdims=True)
    centred = hidden - row_mean
    factor = lax.rsqrt(jnp.mean(centred * centred, axis=-1, keepdims=True) + EPSILON)
    normed = centred * factor
    return (normed * gain_vec + bias_add, normed, factor)


def norm_back(grad_in, normed, factor, gain_vec):
    scaled = grad_in * gain_vec
    return factor * (
        scaled
        - jnp.mean(scaled, axis=-1, keepdims=True)
        - normed * jnp.mean(scaled * normed, axis=-1, keepdims=True)
    )


def per_device(
    tokens,
    doc_blocks,
    pad_tokens,
    w_qkv,
    bias_query,
    bias_value,
    w_attn_out,
    bias_attn_out,
    gain_one,
    shift_one,
    w_up,
    bias_up,
    w_down,
    bias_down,
    gain_two,
    shift_two,
    cotangent,
):
    contexts = lax.axis_size("context")
    row_count = tokens.shape[0]
    share_rows = row_count // lax.axis_size("tensor")
    share_start = lax.axis_index("tensor") * share_rows
    slots = row_count // BLK
    group_rows = row_count * contexts
    window = MAXB * BLK
    per_step = QB // BLK
    step_count = slots // per_step
    start_here = lax.axis_index("context") * row_count
    doc_row = doc_blocks[0]
    pad_row = pad_tokens[0]
    doc_ends = jnp.cumsum(doc_row) * BLK
    doc_starts = doc_ends - doc_row * BLK
    own_places = block_place(start_here + jnp.arange(row_count, dtype=jnp.int32), contexts)
    own_doc, own_live = doc_of(doc_row, pad_row, own_places)
    slot_first = own_places.reshape(slots, BLK)[:, 0]
    slot_doc = jnp.sum((slot_first[:, None] >= doc_ends[None, :]).astype(jnp.int32), axis=1)
    chosen = slot_doc[:, None] == jnp.arange(doc_ends.shape[0], dtype=jnp.int32)[None, :]
    own_begin = jnp.minimum(
        jnp.sum(jnp.where(chosen, doc_starts[None, :], 0), axis=1), group_rows - window
    )
    window_places = (own_begin[:, None] + jnp.arange(window, dtype=jnp.int32)[None, :]).reshape(-1)
    win_doc, win_live = doc_of(doc_row, pad_row, window_places)
    win_doc = win_doc.reshape(slots, window)
    win_live = win_live.reshape(slots, window)
    own_doc_slots = own_doc.reshape(slots, BLK)

    def position_order(gathered):
        rest = gathered.shape[1:]
        return jnp.swapaxes(gathered.reshape((contexts, slots, BLK) + rest), 0, 1).reshape(
            (group_rows,) + rest
        )

    def windows(source, begins):
        return jax.vmap(lambda begin: lax.dynamic_slice_in_dim(source, begin, window, 0))(begins)

    full_qkv, full_out, full_up, full_down = (
        lax.all_gather(w_qkv, ("fsdp", "context"), axis=0, tiled=True),
        lax.all_gather(w_attn_out, ("fsdp", "context"), axis=1, tiled=True),
        lax.all_gather(w_up, ("fsdp", "context"), axis=0, tiled=True),
        lax.all_gather(w_down, ("fsdp", "context"), axis=1, tiled=True),
    )
    inner_width = w_qkv.shape[2]
    heads_here = inner_width // HEAD
    score_scale = HEAD ** (-0.5)
    head_shape = (row_count, heads_here, HEAD)
    slot_shape = (slots, BLK, heads_here, HEAD)
    bias_three = jnp.stack([bias_query, jnp.zeros_like(bias_query), bias_value])
    qkv_low = (
        jnp.einsum("td,dce->tce", tokens, full_qkv, preferred_element_type=jnp.float32) + bias_three
    ).astype(jnp.bfloat16)
    query_low = qkv_low[:, 0].reshape(head_shape)
    key_low = qkv_low[:, 1].reshape(head_shape)
    value_low = qkv_low[:, 2].reshape(head_shape)
    query_slots = query_low.reshape(slot_shape)
    key_all, value_all = (
        lax.all_gather(key_low, "context", axis=0, tiled=True),
        lax.all_gather(value_low, "context", axis=0, tiled=True),
    )
    key_pos = position_order(key_all)
    value_pos = position_order(value_all)

    def slot_scores(query_part, key_part, query_doc, key_doc, key_live):
        raw = (
            jnp.einsum("sqhd,skhd->sqhk", query_part, key_part, preferred_element_type=jnp.float32)
            * score_scale
        )
        allowed = ((query_doc[:, :, None] == key_doc[:, None, :]) & key_live[:, None, :])[
            :, :, None, :
        ]
        return (jnp.where(allowed, raw, MASKED), allowed)

    def forward_step(step):
        key_part = windows(key_pos, own_begin)
        value_part = windows(value_pos, own_begin)
        scores, allowed = slot_scores(query_slots, key_part, own_doc_slots, win_doc, win_live)
        top = jnp.max(scores, axis=3)
        total = jnp.sum(jnp.where(allowed, jnp.exp(scores - top[:, :, :, None]), 0.0), axis=3)
        log_part = top + jnp.log(total)
        prob_low = jnp.where(allowed, jnp.exp(scores - log_part[:, :, :, None]), 0.0).astype(
            jnp.bfloat16
        )
        return (
            jnp.einsum("sqhk,skhd->sqhd", prob_low, value_part, preferred_element_type=jnp.float32),
            log_part,
        )

    attended_steps, log_steps = lax.map(forward_step, jnp.arange(step_count, dtype=jnp.int32))
    attended = attended_steps.reshape(head_shape)
    log_total = log_steps.reshape(row_count, heads_here)
    attended_low = attended.reshape(row_count, inner_width).astype(jnp.bfloat16)
    branch_share = (
        lax.psum_scatter(
            jnp.dot(attended_low, full_out, preferred_element_type=jnp.float32).astype(
                jnp.bfloat16
            ),
            "tensor",
            scatter_dimension=0,
            tiled=True,
        ).astype(jnp.float32)
        + bias_attn_out
    )
    token_share = lax.dynamic_slice_in_dim(tokens, share_start, share_rows, 0).astype(jnp.float32)
    first_share, normed_one_share, factor_one_share = layer_norm(
        token_share + branch_share, gain_one, shift_one
    )
    first, normed_one, factor_one = (
        lax.all_gather(first_share.astype(jnp.bfloat16), "tensor", axis=0, tiled=True).astype(
            first_share.dtype
        ),
        lax.all_gather(normed_one_share.astype(jnp.bfloat16), "tensor", axis=0, tiled=True).astype(
            normed_one_share.dtype
        ),
        lax.all_gather(factor_one_share.astype(jnp.bfloat16), "tensor", axis=0, tiled=True).astype(
            factor_one_share.dtype
        ),
    )
    first_low = first.astype(jnp.bfloat16)
    pre = jnp.dot(first_low, full_up, preferred_element_type=jnp.float32) + bias_up
    act, gelu_back = jax.vjp(lambda hidden: jax.nn.gelu(hidden, approximate=False), pre)
    act_low = act.astype(jnp.bfloat16)
    feed_share = (
        lax.psum_scatter(
            jnp.dot(act_low, full_down, preferred_element_type=jnp.float32).astype(jnp.bfloat16),
            "tensor",
            scatter_dimension=0,
            tiled=True,
        ).astype(jnp.float32)
        + bias_down
    )
    out_share, normed_two_share, factor_two_share = layer_norm(
        first_share + feed_share, gain_two, shift_two
    )
    result_out, normed_two, factor_two = (
        lax.all_gather(out_share.astype(jnp.bfloat16), "tensor", axis=0, tiled=True).astype(
            out_share.dtype
        ),
        lax.all_gather(normed_two_share.astype(jnp.bfloat16), "tensor", axis=0, tiled=True).astype(
            normed_two_share.dtype
        ),
        lax.all_gather(factor_two_share.astype(jnp.bfloat16), "tensor", axis=0, tiled=True).astype(
            factor_two_share.dtype
        ),
    )
    output = result_out.astype(jnp.bfloat16)
    grad_out = cotangent.astype(jnp.float32)
    grad_gain_two = jnp.sum(grad_out * normed_two, axis=0)
    grad_shift_two = jnp.sum(grad_out, axis=0)
    grad_second = norm_back(grad_out, normed_two, factor_two, gain_two)
    grad_feed = grad_second.astype(jnp.bfloat16)
    grad_bias_down = jnp.sum(grad_feed.astype(jnp.float32), axis=0)
    grad_w_down = jnp.einsum("tf,td->fd", act_low, grad_feed, preferred_element_type=jnp.float32)
    grad_act = jnp.einsum("td,fd->tf", grad_feed, full_down, preferred_element_type=jnp.float32)
    grad_pre = gelu_back(grad_act)[0].astype(jnp.bfloat16)
    grad_bias_up = jnp.sum(grad_pre.astype(jnp.float32), axis=0)
    grad_w_up = jnp.einsum("td,tf->df", first_low, grad_pre, preferred_element_type=jnp.float32)
    grad_first = grad_second + lax.psum(
        jnp.einsum("tf,df->td", grad_pre, full_up, preferred_element_type=jnp.float32).astype(
            jnp.bfloat16
        ),
        "tensor",
    ).astype(jnp.float32)
    grad_gain_one = jnp.sum(grad_first * normed_one, axis=0)
    grad_shift_one = jnp.sum(grad_first, axis=0)
    grad_mid = norm_back(grad_first, normed_one, factor_one, gain_one)
    grad_branch = grad_mid.astype(jnp.bfloat16)
    grad_bias_attn_out = jnp.sum(grad_branch.astype(jnp.float32), axis=0)
    grad_w_attn_out = jnp.einsum(
        "te,td->ed", attended_low, grad_branch, preferred_element_type=jnp.float32
    )
    grad_att = (
        jnp.einsum("td,ed->te", grad_branch, full_out, preferred_element_type=jnp.float32)
        .astype(jnp.bfloat16)
        .reshape(head_shape)
    )
    row_delta = jnp.sum(grad_att.astype(jnp.float32) * attended, axis=2)
    grad_slots = grad_att.reshape(slot_shape)
    delta_slots = row_delta.reshape(slots, BLK, heads_here)
    log_slots = log_total.reshape(slots, BLK, heads_here)

    def pair_terms(
        query_part,
        grad_part,
        query_doc,
        query_log,
        query_delta,
        key_part,
        value_part,
        key_doc,
        key_live,
    ):
        scores, allowed = slot_scores(query_part, key_part, query_doc, key_doc, key_live)
        prob = jnp.where(allowed, jnp.exp(scores - query_log[:, :, :, None]), 0.0)
        grad_prob = jnp.einsum(
            "sqhd,skhd->sqhk", grad_part, value_part, preferred_element_type=jnp.float32
        )
        grad_score = (prob * (grad_prob - query_delta[:, :, :, None])).astype(jnp.bfloat16)
        return (prob.astype(jnp.bfloat16), grad_score)

    def query_side():
        key_part = windows(key_pos, own_begin)
        value_part = windows(value_pos, own_begin)
        prob_low, grad_score = pair_terms(
            query_slots,
            grad_slots,
            own_doc_slots,
            log_slots,
            delta_slots,
            key_part,
            value_part,
            win_doc,
            win_live,
        )
        grad_query = (
            jnp.einsum("sqhk,skhd->sqhd", grad_score, key_part, preferred_element_type=jnp.float32)
            * score_scale
        )
        return (own_begin, query_slots, grad_slots, prob_low, grad_score, grad_query)

    def back_step(key_terms, step):
        begins, query_part, grad_part, prob_low, grad_score, grad_query = query_side()
        grad_key = (
            jnp.einsum(
                "sqhk,sqhd->skhd", grad_score, query_part, preferred_element_type=jnp.float32
            )
            * score_scale
        )
        grad_value = jnp.einsum(
            "sqhk,sqhd->skhd", prob_low, grad_part, preferred_element_type=jnp.float32
        )
        terms = jnp.stack([grad_key, grad_value], axis=2)
        for index in range(per_step):
            earlier = lax.dynamic_slice_in_dim(key_terms, begins[index], window, 0)
            key_terms = lax.dynamic_update_slice_in_dim(
                key_terms, earlier + terms[index], begins[index], 0
            )
        return (key_terms, grad_query)

    empty_terms = jnp.zeros((group_rows, 2, heads_here, HEAD), jnp.float32)
    key_terms, query_steps = lax.scan(
        back_step, empty_terms, jnp.arange(step_count, dtype=jnp.int32)
    )
    grad_query = query_steps.reshape(head_shape)
    rest = key_terms.shape[1:]
    own_terms = lax.psum_scatter(
        jnp.swapaxes(key_terms.reshape((slots, contexts, BLK) + rest), 0, 1)
        .reshape((group_rows,) + rest)
        .astype(jnp.bfloat16),
        "context",
        scatter_dimension=0,
        tiled=True,
    ).astype(jnp.float32)
    grad_key = own_terms[:, 0]
    grad_value = own_terms[:, 1]
    grad_qkv = (
        jnp.stack([grad_query, grad_key, grad_value], axis=1)
        .reshape(row_count, 3, inner_width)
        .astype(jnp.bfloat16)
    )
    grad_bias_query = jnp.sum(grad_qkv[:, 0].astype(jnp.float32), axis=0)
    grad_bias_value = jnp.sum(grad_qkv[:, 2].astype(jnp.float32), axis=0)
    grad_w_qkv = jnp.einsum("td,tce->dce", tokens, grad_qkv, preferred_element_type=jnp.float32)
    grad_tokens = grad_mid + lax.psum(
        jnp.einsum("tce,dce->td", grad_qkv, full_qkv, preferred_element_type=jnp.float32).astype(
            jnp.bfloat16
        ),
        "tensor",
    ).astype(jnp.float32)
    shard_qkv, shard_out, shard_up, shard_down = (
        lax.psum_scatter(
            grad_w_qkv.astype(jnp.bfloat16), ("fsdp", "context"), scatter_dimension=0, tiled=True
        ).astype(jnp.float32),
        lax.psum_scatter(
            grad_w_attn_out.astype(jnp.bfloat16),
            ("fsdp", "context"),
            scatter_dimension=1,
            tiled=True,
        ).astype(jnp.float32),
        lax.psum_scatter(
            grad_w_up.astype(jnp.bfloat16), ("fsdp", "context"), scatter_dimension=0, tiled=True
        ).astype(jnp.float32),
        lax.psum_scatter(
            grad_w_down.astype(jnp.bfloat16), ("fsdp", "context"), scatter_dimension=1, tiled=True
        ).astype(jnp.float32),
    )
    small_sums = lax.psum(
        (
            grad_bias_query,
            grad_bias_value,
            grad_bias_attn_out,
            grad_gain_one,
            grad_shift_one,
            grad_bias_up,
            grad_bias_down,
            grad_gain_two,
            grad_shift_two,
        ),
        ("fsdp", "context"),
    )
    return (
        output,
        grad_tokens,
        shard_qkv,
        small_sums[0],
        small_sums[1],
        shard_out,
        small_sums[2],
        small_sums[3],
        small_sums[4],
        shard_up,
        small_sums[5],
        shard_down,
        small_sums[6],
        small_sums[7],
        small_sums[8],
    )


MESH = pl.DeviceIdType.MESH
CHUNK = 512
VMEM_LIMIT = 48 * 1024 * 1024


def ring_place(context, depth):
    z, x = context // 2, context % 2
    return z + x * (2 * depth - 1 - 2 * z)


def ring_context(place, depth):
    x = place // depth
    z = place + x * (2 * depth - 1 - 2 * place)
    return 2 * z + x


def ring_facts(contexts):
    depth = contexts // 2
    fsdp, context = lax.axis_index("fsdp"), lax.axis_index("context")
    place = ring_place(context, depth)

    def at(offset):
        return ring_context((place + offset + 2 * contexts) % contexts, depth)

    return fsdp, context, at


def greet(targets):
    barrier = pltpu.get_barrier_semaphore()
    for target in targets:
        pl.semaphore_signal(barrier, inc=1, device_id=target, device_id_type=MESH)
    pl.semaphore_wait(barrier, len(targets))


def gather_kernel(contexts, count, *refs):
    shards, fulls = refs[:count], refs[count : 2 * count]
    local_sem, send_sem, recv_sem, pair_send, pair_recv = refs[2 * count :]
    fsdp, context, at = ring_facts(contexts)
    half = shards[0].shape[0] // 2
    toward = ({"context": at(1)}, {"context": at(-1)})
    pair = {"fsdp": 1 - fsdp}
    greet([toward[0], toward[1], pair])

    def own(index):
        return pltpu.make_async_copy(
            shards[index], fulls[index].at[fsdp * contexts + context], local_sem.at[index]
        )

    def piece(index, way, step):
        block = fsdp * contexts + at(-step if way == 0 else step)
        return fulls[index].at[block, pl.ds(way * half, half)]

    def hop(index, way, step):
        ref = piece(index, way, step)
        return pltpu.make_async_remote_copy(
            src_ref=ref,
            dst_ref=ref,
            send_sem=send_sem.at[step, index, way],
            recv_sem=recv_sem.at[step, index, way],
            device_id=toward[way],
            device_id_type=MESH,
        )

    def arrival(index, way, step):
        ref = piece(index, way, step + 1)
        return pltpu.make_async_remote_copy(
            src_ref=ref,
            dst_ref=ref,
            send_sem=send_sem.at[step, index, way],
            recv_sem=recv_sem.at[step, index, way],
            device_id=toward[way],
            device_id_type=MESH,
        )

    def across(index, way, step):
        ref = piece(index, way, step)
        return pltpu.make_async_remote_copy(
            src_ref=ref,
            dst_ref=ref,
            send_sem=pair_send.at[step, index, way],
            recv_sem=pair_recv.at[step, index, way],
            device_id=pair,
            device_id_type=MESH,
        )

    def across_arrival(index, way, step):
        block = (1 - fsdp) * contexts + at(-step if way == 0 else step)
        ref = fulls[index].at[block, pl.ds(way * half, half)]
        return pltpu.make_async_remote_copy(
            src_ref=ref,
            dst_ref=ref,
            send_sem=pair_send.at[step, index, way],
            recv_sem=pair_recv.at[step, index, way],
            device_id=pair,
            device_id_type=MESH,
        )

    for index in range(count):
        own(index).start()
    for index in range(count):
        own(index).wait()
        for way in range(2):
            hop(index, way, 0).start()
            across(index, way, 0).start()

    def onward(step, carry):
        for index in range(count):
            for way in range(2):
                arrival(index, way, step - 1).wait_recv()
                hop(index, way, step).start()
                across(index, way, step).start()
        return carry

    lax.fori_loop(1, contexts - 1, onward, 0)
    for index in range(count):
        for way in range(2):
            arrival(index, way, contexts - 2).wait_recv()
            across(index, way, contexts - 1).start()

    def finish(step, carry):
        for index in range(count):
            for way in range(2):
                across(index, way, step).wait_send()
                across_arrival(index, way, step).wait_recv()
        return carry

    def finish_hop(step, carry):
        for index in range(count):
            for way in range(2):
                hop(index, way, step).wait_send()
        return carry

    lax.fori_loop(0, contexts - 1, finish_hop, 0)
    lax.fori_loop(0, contexts, finish, 0)


def gather_rows(shards, contexts, collective_id):
    count = len(shards)
    fulls = pl.pallas_call(
        functools.partial(gather_kernel, contexts, count),
        out_shape=[
            jax.ShapeDtypeStruct((2 * contexts,) + shard.shape, shard.dtype) for shard in shards
        ],
        in_specs=[pl.BlockSpec(memory_space=pl.ANY)] * count,
        out_specs=[pl.BlockSpec(memory_space=pl.ANY)] * count,
        scratch_shapes=[
            pltpu.SemaphoreType.DMA((count,)),
            pltpu.SemaphoreType.DMA((contexts - 1, count, 2)),
            pltpu.SemaphoreType.DMA((contexts - 1, count, 2)),
            pltpu.SemaphoreType.DMA((contexts, count, 2)),
            pltpu.SemaphoreType.DMA((contexts, count, 2)),
        ],
        compiler_params=pltpu.CompilerParams(collective_id=collective_id, has_side_effects=True),
        name="gather_rows",
    )(*shards)
    return [full.reshape(-1, full.shape[-1]) for full in fulls]


def scatter_kernel(contexts, count, *refs):
    grads, small = refs[:count], refs[count]
    outs, small_out = refs[count + 1 : 2 * count + 1], refs[2 * count + 1]
    rest = refs[2 * count + 2 :]
    pairs, slots, small_in = rest[:count], rest[count : 2 * count], rest[2 * count]
    small_now = rest[2 * count + 1]
    send_sem, recv_sem, pair_send, pair_recv, small_send, small_recv = rest[2 * count + 2 :]
    fsdp, context, at = ring_facts(contexts)
    half = outs[0].shape[0] // 2
    toward = ({"context": at(1)}, {"context": at(-1)})
    pair = {"fsdp": 1 - fsdp}
    steps = []
    width = 1
    while width < contexts:
        steps.append({"context": context + width - 2 * width * ((context // width) % 2)})
        width *= 2
    partners = [pair] + steps
    greet([toward[0], toward[1]] + partners)

    def rows(way):
        return pl.ds(way * half, half)

    def block_at(way, step):
        return at(-1 - step if way == 0 else 1 + step)

    def across(index, way, step):
        block = block_at(way, step)
        return pltpu.make_async_remote_copy(
            src_ref=grads[index].at[1 - fsdp, block, rows(way)],
            dst_ref=pairs[index].at[block, rows(way)],
            send_sem=pair_send.at[step, index, way],
            recv_sem=pair_recv.at[step, index, way],
            device_id=pair,
            device_id_type=MESH,
        )

    def hop(index, way, step):
        return pltpu.make_async_remote_copy(
            src_ref=pairs[index].at[block_at(way, step), rows(way)],
            dst_ref=slots[index].at[step, rows(way)],
            send_sem=send_sem.at[step, index, way],
            recv_sem=recv_sem.at[step, index, way],
            device_id=toward[way],
            device_id_type=MESH,
        )

    def small_hop(step):
        return pltpu.make_async_remote_copy(
            src_ref=small_now.at[step],
            dst_ref=small_in.at[step],
            send_sem=small_send.at[step],
            recv_sem=small_recv.at[step],
            device_id=partners[step],
            device_id_type=MESH,
        )

    def pair_sum(index, way, step):
        across(index, way, step).wait_recv()
        block = block_at(way, step)
        return grads[index][fsdp, block, rows(way)].astype(jnp.float32) + pairs[index][
            block, rows(way)
        ].astype(jnp.float32)

    small_now[0] = small[...]
    small_hop(0).start()

    def offer(step, carry):
        for index in range(count):
            for way in range(2):
                across(index, way, step).start()
        return carry

    lax.fori_loop(0, contexts, offer, 0)

    for index in range(count):
        for way in range(2):
            total = pair_sum(index, way, 0)
            pairs[index][block_at(way, 0), rows(way)] = total.astype(jnp.bfloat16)
            hop(index, way, 0).start()

    for step in range(len(partners)):
        small_hop(step).wait()
        total = small_now[step] + small_in[step]
        if step + 1 < len(partners):
            small_now[step + 1] = total
            small_hop(step + 1).start()
        else:
            small_out[...] = total

    def onward(step, carry):
        for index in range(count):
            for way in range(2):
                total = pair_sum(index, way, step)
                hop(index, way, step - 1).wait_recv()
                total = total + slots[index][step - 1, rows(way)].astype(jnp.float32)
                pairs[index][block_at(way, step), rows(way)] = total.astype(jnp.bfloat16)
                hop(index, way, step).start()
        return carry

    lax.fori_loop(1, contexts - 1, onward, 0)
    for index in range(count):
        for way in range(2):
            total = pair_sum(index, way, contexts - 1)
            hop(index, way, contexts - 2).wait_recv()
            outs[index][rows(way)] = total + slots[index][contexts - 2, rows(way)].astype(
                jnp.float32
            )

    def finish(step, carry):
        for index in range(count):
            for way in range(2):
                across(index, way, step).wait_send()
        return carry

    def finish_hop(step, carry):
        for index in range(count):
            for way in range(2):
                hop(index, way, step).wait_send()
        return carry

    lax.fori_loop(0, contexts, finish, 0)
    lax.fori_loop(0, contexts - 1, finish_hop, 0)


def scatter_rows(grads, small, contexts, collective_id):
    count = len(grads)
    rows = grads[0].shape[0] // (2 * contexts)
    widths = [grad.shape[1] for grad in grads]
    doubling = 1 + (contexts - 1).bit_length()
    vmem = pl.BlockSpec(memory_space=pltpu.VMEM)
    return pl.pallas_call(
        functools.partial(scatter_kernel, contexts, count),
        out_shape=[jax.ShapeDtypeStruct((rows, width), jnp.float32) for width in widths]
        + [jax.ShapeDtypeStruct(small.shape, jnp.float32)],
        in_specs=[vmem] * (count + 1),
        out_specs=[vmem] * (count + 1),
        scratch_shapes=[pltpu.VMEM((contexts, rows, width), jnp.bfloat16) for width in widths]
        + [pltpu.VMEM((contexts - 1, rows, width), jnp.bfloat16) for width in widths]
        + [
            pltpu.VMEM((doubling,) + small.shape, jnp.float32),
            pltpu.VMEM((doubling,) + small.shape, jnp.float32),
            pltpu.SemaphoreType.DMA((contexts - 1, count, 2)),
            pltpu.SemaphoreType.DMA((contexts - 1, count, 2)),
            pltpu.SemaphoreType.DMA((contexts, count, 2)),
            pltpu.SemaphoreType.DMA((contexts, count, 2)),
            pltpu.SemaphoreType.DMA((doubling,)),
            pltpu.SemaphoreType.DMA((doubling,)),
        ],
        compiler_params=pltpu.CompilerParams(
            collective_id=collective_id, has_side_effects=True, vmem_limit_bytes=VMEM_LIMIT
        ),
        name="scatter_rows",
    )(*[grad.reshape(2, contexts, rows, grad.shape[1]) for grad in grads], small)


def swap_kernel(contexts, to_heads, source, result, local_sem, send_sem, recv_sem):
    context = lax.axis_index("context")
    others = [(context + shift) % contexts for shift in range(1, contexts)]
    greet([{"context": other} for other in others])

    def ends(there):
        if to_heads:
            return source.at[there], result.at[:, context]
        return source.at[:, there], result.at[context]

    here, mine = ends(context)
    keep = pltpu.make_async_copy(here, mine, local_sem)
    copies = []
    for index, other in enumerate(others):
        sent, landed = ends(other)
        copies.append(
            pltpu.make_async_remote_copy(
                src_ref=sent,
                dst_ref=landed,
                send_sem=send_sem.at[index],
                recv_sem=recv_sem.at[index],
                device_id={"context": other},
                device_id_type=MESH,
            )
        )
    for copy in copies:
        copy.start()
    keep.start()
    keep.wait()
    for copy in copies:
        copy.wait()


def swap(source, contexts, to_heads, collective_id):
    shape = (source.shape[1], source.shape[0]) + source.shape[2:]
    return pl.pallas_call(
        functools.partial(swap_kernel, contexts, to_heads),
        out_shape=jax.ShapeDtypeStruct(shape, source.dtype),
        in_specs=[pl.BlockSpec(memory_space=pl.ANY)],
        out_specs=pl.BlockSpec(memory_space=pl.ANY),
        scratch_shapes=[
            pltpu.SemaphoreType.DMA(()),
            pltpu.SemaphoreType.DMA((contexts - 1,)),
            pltpu.SemaphoreType.DMA((contexts - 1,)),
        ],
        compiler_params=pltpu.CompilerParams(collective_id=collective_id, has_side_effects=True),
        name="swap_heads" if to_heads else "swap_rows",
    )(source)


def turned(block):
    return block.astype(jnp.float32).T.astype(jnp.bfloat16)


def key_mask(scores, first_key, low, high):
    keys = first_key + lax.broadcasted_iota(jnp.int32, scores.shape, 0)
    return jnp.where((keys >= low) & (keys < high), scores, MASKED)


def attend_kernel(meta, qkv, att, att_wide, log_total, keys, values, held):
    blocks = qkv.shape[0]
    window = held.shape[0]

    def lay(block, carry):
        place = pl.ds(pl.multiple_of(block * BLK, BLK), BLK)
        keys[place, :] = turned(qkv[block, HEAD : 2 * HEAD])
        values[:, place] = qkv[block, 2 * HEAD : 3 * HEAD]
        return carry

    lax.fori_loop(0, blocks, lay, 0)

    def one(block, carry):
        begin, low, high = meta[0, block], meta[1, block], meta[2, block]
        query = qkv[block, 0:HEAD]
        top = jnp.full((1, BLK), MASKED, jnp.float32)
        for part in range(0, window, CHUNK):
            place = pl.ds(pl.multiple_of(begin + part, BLK), CHUNK)
            scores = jnp.dot(keys[place, :], query, preferred_element_type=jnp.float32)
            scores = key_mask(scores, begin + part, low, high)
            held[part : part + CHUNK] = scores
            top = jnp.maximum(top, jnp.max(scores, axis=0, keepdims=True))
        total = jnp.zeros((1, BLK), jnp.float32)
        out = jnp.zeros((HEAD, BLK), jnp.float32)
        for part in range(0, window, CHUNK):
            place = pl.ds(pl.multiple_of(begin + part, BLK), CHUNK)
            prob = jnp.exp(held[part : part + CHUNK] - top)
            total += jnp.sum(prob, axis=0, keepdims=True)
            out += jnp.dot(
                values[:, place], prob.astype(jnp.bfloat16), preferred_element_type=jnp.float32
            )
        out = out / total
        att_wide[block] = out
        att[block] = out.astype(jnp.bfloat16)
        log_total[block] = top + jnp.log(total)
        return carry

    lax.fori_loop(0, blocks, one, 0)


def attend(meta, qkv):
    blocks = qkv.shape[0]
    rows = blocks * BLK
    vmem = pl.BlockSpec(memory_space=pltpu.VMEM)
    return pl.pallas_call(
        attend_kernel,
        out_shape=[
            jax.ShapeDtypeStruct((blocks, HEAD, BLK), jnp.bfloat16),
            jax.ShapeDtypeStruct((blocks, HEAD, BLK), jnp.float32),
            jax.ShapeDtypeStruct((blocks, 1, BLK), jnp.float32),
        ],
        in_specs=[pl.BlockSpec(memory_space=pltpu.SMEM), vmem],
        out_specs=[vmem] * 3,
        scratch_shapes=[
            pltpu.VMEM((rows, HEAD), jnp.bfloat16),
            pltpu.VMEM((HEAD, rows), jnp.bfloat16),
            pltpu.VMEM((MAXB * BLK, BLK), jnp.float32),
        ],
        compiler_params=pltpu.CompilerParams(vmem_limit_bytes=VMEM_LIMIT),
        name="attend",
    )(meta, qkv)


def attend_back_kernel(
    meta, qkv, grad_att, att_wide, log_total, grads, keys, keys_turned, values, grad_k, grad_v
):
    blocks = qkv.shape[0]
    window = MAXB * BLK

    def lay(block, carry):
        place = pl.ds(pl.multiple_of(block * BLK, BLK), BLK)
        keys[place, :] = turned(qkv[block, HEAD : 2 * HEAD])
        keys_turned[:, place] = qkv[block, HEAD : 2 * HEAD]
        values[place, :] = turned(qkv[block, 2 * HEAD : 3 * HEAD])
        grad_k[place, :] = jnp.zeros((BLK, HEAD), jnp.float32)
        grad_v[place, :] = jnp.zeros((BLK, HEAD), jnp.float32)
        return carry

    lax.fori_loop(0, blocks, lay, 0)

    def one(block, carry):
        begin, low, high = meta[0, block], meta[1, block], meta[2, block]
        query = qkv[block, 0:HEAD]
        grad = grad_att[block]
        query_rows = turned(query)
        grad_rows = turned(grad)
        delta = jnp.sum(grad.astype(jnp.float32) * att_wide[block], axis=0, keepdims=True)
        log_row = log_total[block]
        grad_q = jnp.zeros((HEAD, BLK), jnp.float32)
        for part in range(0, window, CHUNK):
            place = pl.ds(pl.multiple_of(begin + part, BLK), CHUNK)
            scores = jnp.dot(keys[place, :], query, preferred_element_type=jnp.float32)
            prob = jnp.exp(key_mask(scores, begin + part, low, high) - log_row)
            grad_prob = jnp.dot(values[place, :], grad, preferred_element_type=jnp.float32)
            grad_score = (prob * (grad_prob - delta)).astype(jnp.bfloat16)
            grad_q += jnp.dot(
                keys_turned[:, place], grad_score, preferred_element_type=jnp.float32
            )
            grad_k[place, :] += jnp.dot(grad_score, query_rows, preferred_element_type=jnp.float32)
            grad_v[place, :] += jnp.dot(
                prob.astype(jnp.bfloat16), grad_rows, preferred_element_type=jnp.float32
            )
        grads[block, 0:HEAD] = (grad_q * HEAD ** (-0.5)).astype(jnp.bfloat16)
        return carry

    lax.fori_loop(0, blocks, one, 0)

    def store(block, carry):
        place = pl.ds(pl.multiple_of(block * BLK, BLK), BLK)
        grads[block, HEAD : 2 * HEAD] = grad_k[place, :].T.astype(jnp.bfloat16)
        grads[block, 2 * HEAD : 3 * HEAD] = grad_v[place, :].T.astype(jnp.bfloat16)
        return carry

    lax.fori_loop(0, blocks, store, 0)


def attend_back(meta, qkv, grad_att, att_wide, log_total):
    blocks = qkv.shape[0]
    rows = blocks * BLK
    vmem = pl.BlockSpec(memory_space=pltpu.VMEM)
    return pl.pallas_call(
        attend_back_kernel,
        out_shape=jax.ShapeDtypeStruct(qkv.shape, jnp.bfloat16),
        in_specs=[pl.BlockSpec(memory_space=pltpu.SMEM)] + [vmem] * 4,
        out_specs=vmem,
        scratch_shapes=[
            pltpu.VMEM((rows, HEAD), jnp.bfloat16),
            pltpu.VMEM((HEAD, rows), jnp.bfloat16),
            pltpu.VMEM((rows, HEAD), jnp.bfloat16),
            pltpu.VMEM((rows, HEAD), jnp.float32),
            pltpu.VMEM((rows, HEAD), jnp.float32),
        ],
        compiler_params=pltpu.CompilerParams(vmem_limit_bytes=VMEM_LIMIT),
        name="attend_back",
    )(meta, qkv, grad_att, att_wide, log_total)


def over_tensor(low):
    other = lax.ppermute(low, "tensor", [(0, 1), (1, 0)])
    return low.astype(jnp.float32) + other.astype(jnp.float32)


def ring_device(
    tokens,
    doc_blocks,
    pad_tokens,
    w_qkv,
    bias_query,
    bias_value,
    w_attn_out,
    bias_attn_out,
    gain_one,
    shift_one,
    w_up,
    bias_up,
    w_down,
    bias_down,
    gain_two,
    shift_two,
    cotangent,
):
    contexts = lax.axis_size("context")
    row_count, width = tokens.shape
    slots = row_count // BLK
    inner_width = w_qkv.shape[2]
    heads_here = inner_width // HEAD
    blocks = slots * contexts
    wide = functools.partial(jnp.einsum, preferred_element_type=jnp.float32)

    doc_ends = jnp.cumsum(doc_blocks[0]) * BLK
    firsts = jnp.arange(blocks, dtype=jnp.int32) * BLK
    doc_of_block = jnp.sum((firsts[:, None] >= doc_ends[None, :]).astype(jnp.int32), axis=1)
    chosen = doc_of_block[:, None] == jnp.arange(doc_ends.shape[0], dtype=jnp.int32)[None, :]
    low = jnp.sum(jnp.where(chosen, doc_ends - doc_blocks[0] * BLK, 0), axis=1)
    high = jnp.sum(jnp.where(chosen, doc_ends - pad_tokens[0], 0), axis=1)
    begin = jnp.minimum(low, (blocks - MAXB) * BLK)
    meta = jnp.stack([begin, low, high]).astype(jnp.int32)

    full_qkv, full_out, full_up, full_down = gather_rows(
        [w_qkv.reshape(w_qkv.shape[0], -1), w_attn_out.T, w_up, w_down.T], contexts, 0
    )

    bias_three = jnp.concatenate([bias_query, jnp.zeros_like(bias_query), bias_value])
    qkv = (wide("td,df->tf", tokens, full_qkv) + bias_three).astype(jnp.bfloat16)
    query_scale = jnp.concatenate(
        [jnp.full((inner_width,), HEAD ** (-0.5)), jnp.ones((2 * inner_width,))]
    ).astype(jnp.bfloat16)
    qkv_heads = (
        (qkv * query_scale)
        .reshape(slots, BLK, 3, heads_here, HEAD)
        .transpose(3, 0, 2, 4, 1)
        .reshape(heads_here, slots, 3 * HEAD, BLK)
    )
    qkv_here = swap(qkv_heads, contexts, True, 1).reshape(blocks, 3 * HEAD, BLK)
    att_low, att_wide, log_total = attend(meta, qkv_here)
    att_back = swap(att_low.reshape(slots, contexts, HEAD, BLK), contexts, False, 2)
    attended_low = att_back.transpose(1, 3, 0, 2).reshape(row_count, inner_width)

    branch = (
        over_tensor(wide("te,de->td", attended_low, full_out).astype(jnp.bfloat16)) + bias_attn_out
    )
    first, normed_one, factor_one = layer_norm(
        tokens.astype(jnp.float32) + branch, gain_one, shift_one
    )
    first_low = first.astype(jnp.bfloat16)
    pre = wide("td,df->tf", first_low, full_up) + bias_up
    act, gelu_back = jax.vjp(lambda hidden: jax.nn.gelu(hidden, approximate=False), pre)
    act_low = act.astype(jnp.bfloat16)
    feed = over_tensor(wide("tf,df->td", act_low, full_down).astype(jnp.bfloat16)) + bias_down
    out, normed_two, factor_two = layer_norm(first + feed, gain_two, shift_two)
    output = out.astype(jnp.bfloat16)

    grad_out = cotangent.astype(jnp.float32)
    grad_gain_two = jnp.sum(grad_out * normed_two, axis=0)
    grad_shift_two = jnp.sum(grad_out, axis=0)
    grad_second = norm_back(grad_out, normed_two, factor_two, gain_two)
    grad_feed = grad_second.astype(jnp.bfloat16)
    grad_bias_down = jnp.sum(grad_feed.astype(jnp.float32), axis=0)
    grad_act = wide("td,df->tf", grad_feed, full_down)
    grad_pre = gelu_back(grad_act)[0].astype(jnp.bfloat16)
    grad_bias_up = jnp.sum(grad_pre.astype(jnp.float32), axis=0)
    grad_first = grad_second + over_tensor(
        wide("tf,df->td", grad_pre, full_up).astype(jnp.bfloat16)
    )
    grad_w_down = wide("td,tf->df", grad_feed, act_low).astype(jnp.bfloat16)
    grad_w_up = wide("td,tf->df", first_low, grad_pre).astype(jnp.bfloat16)
    grad_gain_one = jnp.sum(grad_first * normed_one, axis=0)
    grad_shift_one = jnp.sum(grad_first, axis=0)
    grad_mid = norm_back(grad_first, normed_one, factor_one, gain_one)
    grad_branch = grad_mid.astype(jnp.bfloat16)
    grad_bias_attn_out = jnp.sum(grad_branch.astype(jnp.float32), axis=0)
    grad_w_attn_out = wide("td,te->de", grad_branch, attended_low).astype(jnp.bfloat16)
    grad_att = (
        wide("td,de->te", grad_branch, full_out)
        .astype(jnp.bfloat16)
        .reshape(slots, BLK, heads_here, HEAD)
        .transpose(2, 0, 3, 1)
    )
    grad_att_here = swap(grad_att, contexts, True, 3).reshape(blocks, HEAD, BLK)
    grad_here = attend_back(meta, qkv_here, grad_att_here, att_wide, log_total)
    grad_qkv = (
        swap(grad_here.reshape(slots, contexts, 3 * HEAD, BLK), contexts, False, 4)
        .reshape(heads_here, slots, 3, HEAD, BLK)
        .transpose(1, 4, 2, 0, 3)
        .reshape(row_count, 3 * inner_width)
    )
    grad_bias = jnp.sum(grad_qkv.astype(jnp.float32), axis=0)
    grad_tokens = grad_mid + over_tensor(
        wide("tf,df->td", grad_qkv, full_qkv).astype(jnp.bfloat16)
    )
    grad_w_qkv = wide("td,tf->df", tokens, grad_qkv).astype(jnp.bfloat16)
    smalls = [
        grad_bias[:inner_width],
        grad_bias[2 * inner_width :],
        grad_bias_attn_out,
        grad_gain_one,
        grad_shift_one,
        grad_bias_up,
        grad_bias_down,
        grad_gain_two,
        grad_shift_two,
    ]
    shard_qkv, shard_out, shard_up, shard_down, small_rows = scatter_rows(
        [grad_w_qkv, grad_w_attn_out, grad_w_up, grad_w_down],
        jnp.concatenate(smalls).reshape(-1, 128),
        contexts,
        5,
    )
    flat = small_rows.reshape(-1)
    sums = []
    start = 0
    for small in smalls:
        sums.append(flat[start : start + small.shape[0]])
        start += small.shape[0]
    return (
        output,
        grad_tokens,
        shard_qkv.reshape(w_qkv.shape),
        sums[0],
        sums[1],
        shard_out.T,
        sums[2],
        sums[3],
        sums[4],
        shard_up,
        sums[5],
        shard_down.T,
        sums[6],
        sums[7],
        sums[8],
    )


def solution(mesh):
    in_specs = (
        P(("fsdp", "context"), None),
        P("fsdp", None),
        P("fsdp", None),
        P(("fsdp", "context"), None, "tensor"),
        P("tensor"),
        P("tensor"),
        P("tensor", ("fsdp", "context")),
        P(),
        P(),
        P(),
        P(("fsdp", "context"), "tensor"),
        P("tensor"),
        P("tensor", ("fsdp", "context")),
        P(),
        P(),
        P(),
        P(("fsdp", "context"), None),
    )
    out_specs = (
        P(("fsdp", "context"), None),
        P(("fsdp", "context"), None),
        P(("fsdp", "context"), None, "tensor"),
        P("tensor"),
        P("tensor"),
        P("tensor", ("fsdp", "context")),
        P(),
        P(),
        P(),
        P(("fsdp", "context"), "tensor"),
        P("tensor"),
        P("tensor", ("fsdp", "context")),
        P(),
        P(),
        P(),
    )
    contexts = mesh.shape["context"]
    heads_each = 1024 // HEAD // mesh.shape["tensor"]
    fits = (
        mesh.shape["fsdp"] == 2
        and mesh.shape["tensor"] == 2
        and contexts == 8
        and heads_each == contexts
    )
    return jax.shard_map(
        ring_device if fits else per_device, mesh=mesh, in_specs=in_specs, out_specs=out_specs, check_vma=False
    )
```

```python
import functools

import jax
import jax.numpy as jnp
from jax import lax
from jax.experimental import pallas as pl
from jax.experimental.pallas import tpu as pltpu
from jax.sharding import PartitionSpec as P

HEAD = 64
TOK_DEV = 512
BLK = 128
MAXB = 16
QB = 512


EPSILON = 1e-05
MASKED = -1e30


def block_place(stored, contexts):
    local_row = stored % TOK_DEV
    owner = stored // TOK_DEV
    return (local_row // BLK * contexts + owner) * BLK + local_row % BLK


def doc_of(doc_row, pad_row, positions):
    doc_ends = jnp.cumsum(doc_row) * BLK
    doc_index = jnp.sum((positions[:, None] >= doc_ends[None, :]).astype(jnp.int32), axis=1)
    chosen = doc_index[:, None] == jnp.arange(doc_ends.shape[0], dtype=jnp.int32)[None, :]
    live_end = jnp.sum(jnp.where(chosen, doc_ends - pad_row, 0), axis=1)
    return (doc_index, positions < live_end)


def layer_norm(hidden, gain_vec, bias_add):
    row_mean = jnp.mean(hidden, axis=-1, keepdims=True)
    centred = hidden - row_mean
    factor = lax.rsqrt(jnp.mean(centred * centred, axis=-1, keepdims=True) + EPSILON)
    normed = centred * factor
    return (normed * gain_vec + bias_add, normed, factor)


def norm_back(grad_in, normed, factor, gain_vec):
    scaled = grad_in * gain_vec
    return factor * (
        scaled
        - jnp.mean(scaled, axis=-1, keepdims=True)
        - normed * jnp.mean(scaled * normed, axis=-1, keepdims=True)
    )


def per_device(
    tokens,
    doc_blocks,
    pad_tokens,
    w_qkv,
    bias_query,
    bias_value,
    w_attn_out,
    bias_attn_out,
    gain_one,
    shift_one,
    w_up,
    bias_up,
    w_down,
    bias_down,
    gain_two,
    shift_two,
    cotangent,
):
    contexts = lax.axis_size("context")
    row_count = tokens.shape[0]
    share_rows = row_count // lax.axis_size("tensor")
    share_start = lax.axis_index("tensor") * share_rows
    slots = row_count // BLK
    group_rows = row_count * contexts
    window = MAXB * BLK
    per_step = QB // BLK
    step_count = slots // per_step
    start_here = lax.axis_index("context") * row_count
    doc_row = doc_blocks[0]
    pad_row = pad_tokens[0]
    doc_ends = jnp.cumsum(doc_row) * BLK
    doc_starts = doc_ends - doc_row * BLK
    own_places = block_place(start_here + jnp.arange(row_count, dtype=jnp.int32), contexts)
    own_doc, own_live = doc_of(doc_row, pad_row, own_places)
    slot_first = own_places.reshape(slots, BLK)[:, 0]
    slot_doc = jnp.sum((slot_first[:, None] >= doc_ends[None, :]).astype(jnp.int32), axis=1)
    chosen = slot_doc[:, None] == jnp.arange(doc_ends.shape[0], dtype=jnp.int32)[None, :]
    own_begin = jnp.minimum(
        jnp.sum(jnp.where(chosen, doc_starts[None, :], 0), axis=1), group_rows - window
    )
    window_places = (own_begin[:, None] + jnp.arange(window, dtype=jnp.int32)[None, :]).reshape(-1)
    win_doc, win_live = doc_of(doc_row, pad_row, window_places)
    win_doc = win_doc.reshape(slots, window)
    win_live = win_live.reshape(slots, window)
    own_doc_slots = own_doc.reshape(slots, BLK)

    def position_order(gathered):
        rest = gathered.shape[1:]
        return jnp.swapaxes(gathered.reshape((contexts, slots, BLK) + rest), 0, 1).reshape(
            (group_rows,) + rest
        )

    def windows(source, begins):
        return jax.vmap(lambda begin: lax.dynamic_slice_in_dim(source, begin, window, 0))(begins)

    full_qkv, full_out, full_up, full_down = (
        lax.all_gather(w_qkv, ("fsdp", "context"), axis=0, tiled=True),
        lax.all_gather(w_attn_out, ("fsdp", "context"), axis=1, tiled=True),
        lax.all_gather(w_up, ("fsdp", "context"), axis=0, tiled=True),
        lax.all_gather(w_down, ("fsdp", "context"), axis=1, tiled=True),
    )
    inner_width = w_qkv.shape[2]
    heads_here = inner_width // HEAD
    score_scale = HEAD ** (-0.5)
    head_shape = (row_count, heads_here, HEAD)
    slot_shape = (slots, BLK, heads_here, HEAD)
    bias_three = jnp.stack([bias_query, jnp.zeros_like(bias_query), bias_value])
    qkv_low = (
        jnp.einsum("td,dce->tce", tokens, full_qkv, preferred_element_type=jnp.float32) + bias_three
    ).astype(jnp.bfloat16)
    query_low = qkv_low[:, 0].reshape(head_shape)
    key_low = qkv_low[:, 1].reshape(head_shape)
    value_low = qkv_low[:, 2].reshape(head_shape)
    query_slots = query_low.reshape(slot_shape)
    key_all, value_all = (
        lax.all_gather(key_low, "context", axis=0, tiled=True),
        lax.all_gather(value_low, "context", axis=0, tiled=True),
    )
    key_pos = position_order(key_all)
    value_pos = position_order(value_all)

    def slot_scores(query_part, key_part, query_doc, key_doc, key_live):
        raw = (
            jnp.einsum("sqhd,skhd->sqhk", query_part, key_part, preferred_element_type=jnp.float32)
            * score_scale
        )
        allowed = ((query_doc[:, :, None] == key_doc[:, None, :]) & key_live[:, None, :])[
            :, :, None, :
        ]
        return (jnp.where(allowed, raw, MASKED), allowed)

    def forward_step(step):
        key_part = windows(key_pos, own_begin)
        value_part = windows(value_pos, own_begin)
        scores, allowed = slot_scores(query_slots, key_part, own_doc_slots, win_doc, win_live)
        top = jnp.max(scores, axis=3)
        total = jnp.sum(jnp.where(allowed, jnp.exp(scores - top[:, :, :, None]), 0.0), axis=3)
        log_part = top + jnp.log(total)
        prob_low = jnp.where(allowed, jnp.exp(scores - log_part[:, :, :, None]), 0.0).astype(
            jnp.bfloat16
        )
        return (
            jnp.einsum("sqhk,skhd->sqhd", prob_low, value_part, preferred_element_type=jnp.float32),
            log_part,
        )

    attended_steps, log_steps = lax.map(forward_step, jnp.arange(step_count, dtype=jnp.int32))
    attended = attended_steps.reshape(head_shape)
    log_total = log_steps.reshape(row_count, heads_here)
    attended_low = attended.reshape(row_count, inner_width).astype(jnp.bfloat16)
    branch_share = (
        lax.psum_scatter(
            jnp.dot(attended_low, full_out, preferred_element_type=jnp.float32).astype(
                jnp.bfloat16
            ),
            "tensor",
            scatter_dimension=0,
            tiled=True,
        ).astype(jnp.float32)
        + bias_attn_out
    )
    token_share = lax.dynamic_slice_in_dim(tokens, share_start, share_rows, 0).astype(jnp.float32)
    first_share, normed_one_share, factor_one_share = layer_norm(
        token_share + branch_share, gain_one, shift_one
    )
    first, normed_one, factor_one = (
        lax.all_gather(first_share.astype(jnp.bfloat16), "tensor", axis=0, tiled=True).astype(
            first_share.dtype
        ),
        lax.all_gather(normed_one_share.astype(jnp.bfloat16), "tensor", axis=0, tiled=True).astype(
            normed_one_share.dtype
        ),
        lax.all_gather(factor_one_share.astype(jnp.bfloat16), "tensor", axis=0, tiled=True).astype(
            factor_one_share.dtype
        ),
    )
    first_low = first.astype(jnp.bfloat16)
    pre = jnp.dot(first_low, full_up, preferred_element_type=jnp.float32) + bias_up
    act, gelu_back = jax.vjp(lambda hidden: jax.nn.gelu(hidden, approximate=False), pre)
    act_low = act.astype(jnp.bfloat16)
    feed_share = (
        lax.psum_scatter(
            jnp.dot(act_low, full_down, preferred_element_type=jnp.float32).astype(jnp.bfloat16),
            "tensor",
            scatter_dimension=0,
            tiled=True,
        ).astype(jnp.float32)
        + bias_down
    )
    out_share, normed_two_share, factor_two_share = layer_norm(
        first_share + feed_share, gain_two, shift_two
    )
    result_out, normed_two, factor_two = (
        lax.all_gather(out_share.astype(jnp.bfloat16), "tensor", axis=0, tiled=True).astype(
            out_share.dtype
        ),
        lax.all_gather(normed_two_share.astype(jnp.bfloat16), "tensor", axis=0, tiled=True).astype(
            normed_two_share.dtype
        ),
        lax.all_gather(factor_two_share.astype(jnp.bfloat16), "tensor", axis=0, tiled=True).astype(
            factor_two_share.dtype
        ),
    )
    output = result_out.astype(jnp.bfloat16)
    grad_out = cotangent.astype(jnp.float32)
    grad_gain_two = jnp.sum(grad_out * normed_two, axis=0)
    grad_shift_two = jnp.sum(grad_out, axis=0)
    grad_second = norm_back(grad_out, normed_two, factor_two, gain_two)
    grad_feed = grad_second.astype(jnp.bfloat16)
    grad_bias_down = jnp.sum(grad_feed.astype(jnp.float32), axis=0)
    grad_w_down = jnp.einsum("tf,td->fd", act_low, grad_feed, preferred_element_type=jnp.float32)
    grad_act = jnp.einsum("td,fd->tf", grad_feed, full_down, preferred_element_type=jnp.float32)
    grad_pre = gelu_back(grad_act)[0].astype(jnp.bfloat16)
    grad_bias_up = jnp.sum(grad_pre.astype(jnp.float32), axis=0)
    grad_w_up = jnp.einsum("td,tf->df", first_low, grad_pre, preferred_element_type=jnp.float32)
    grad_first = grad_second + lax.psum(
        jnp.einsum("tf,df->td", grad_pre, full_up, preferred_element_type=jnp.float32).astype(
            jnp.bfloat16
        ),
        "tensor",
    ).astype(jnp.float32)
    grad_gain_one = jnp.sum(grad_first * normed_one, axis=0)
    grad_shift_one = jnp.sum(grad_first, axis=0)
    grad_mid = norm_back(grad_first, normed_one, factor_one, gain_one)
    grad_branch = grad_mid.astype(jnp.bfloat16)
    grad_bias_attn_out = jnp.sum(grad_branch.astype(jnp.float32), axis=0)
    grad_w_attn_out = jnp.einsum(
        "te,td->ed", attended_low, grad_branch, preferred_element_type=jnp.float32
    )
    grad_att = (
        jnp.einsum("td,ed->te", grad_branch, full_out, preferred_element_type=jnp.float32)
        .astype(jnp.bfloat16)
        .reshape(head_shape)
    )
    row_delta = jnp.sum(grad_att.astype(jnp.float32) * attended, axis=2)
    grad_slots = grad_att.reshape(slot_shape)
    delta_slots = row_delta.reshape(slots, BLK, heads_here)
    log_slots = log_total.reshape(slots, BLK, heads_here)

    def pair_terms(
        query_part,
        grad_part,
        query_doc,
        query_log,
        query_delta,
        key_part,
        value_part,
        key_doc,
        key_live,
    ):
        scores, allowed = slot_scores(query_part, key_part, query_doc, key_doc, key_live)
        prob = jnp.where(allowed, jnp.exp(scores - query_log[:, :, :, None]), 0.0)
        grad_prob = jnp.einsum(
            "sqhd,skhd->sqhk", grad_part, value_part, preferred_element_type=jnp.float32
        )
        grad_score = (prob * (grad_prob - query_delta[:, :, :, None])).astype(jnp.bfloat16)
        return (prob.astype(jnp.bfloat16), grad_score)

    def query_side():
        key_part = windows(key_pos, own_begin)
        value_part = windows(value_pos, own_begin)
        prob_low, grad_score = pair_terms(
            query_slots,
            grad_slots,
            own_doc_slots,
            log_slots,
            delta_slots,
            key_part,
            value_part,
            win_doc,
            win_live,
        )
        grad_query = (
            jnp.einsum("sqhk,skhd->sqhd", grad_score, key_part, preferred_element_type=jnp.float32)
            * score_scale
        )
        return (own_begin, query_slots, grad_slots, prob_low, grad_score, grad_query)

    def back_step(key_terms, step):
        begins, query_part, grad_part, prob_low, grad_score, grad_query = query_side()
        grad_key = (
            jnp.einsum(
                "sqhk,sqhd->skhd", grad_score, query_part, preferred_element_type=jnp.float32
            )
            * score_scale
        )
        grad_value = jnp.einsum(
            "sqhk,sqhd->skhd", prob_low, grad_part, preferred_element_type=jnp.float32
        )
        terms = jnp.stack([grad_key, grad_value], axis=2)
        for index in range(per_step):
            earlier = lax.dynamic_slice_in_dim(key_terms, begins[index], window, 0)
            key_terms = lax.dynamic_update_slice_in_dim(
                key_terms, earlier + terms[index], begins[index], 0
            )
        return (key_terms, grad_query)

    empty_terms = jnp.zeros((group_rows, 2, heads_here, HEAD), jnp.float32)
    key_terms, query_steps = lax.scan(
        back_step, empty_terms, jnp.arange(step_count, dtype=jnp.int32)
    )
    grad_query = query_steps.reshape(head_shape)
    rest = key_terms.shape[1:]
    own_terms = lax.psum_scatter(
        jnp.swapaxes(key_terms.reshape((slots, contexts, BLK) + rest), 0, 1)
        .reshape((group_rows,) + rest)
        .astype(jnp.bfloat16),
        "context",
        scatter_dimension=0,
        tiled=True,
    ).astype(jnp.float32)
    grad_key = own_terms[:, 0]
    grad_value = own_terms[:, 1]
    grad_qkv = (
        jnp.stack([grad_query, grad_key, grad_value], axis=1)
        .reshape(row_count, 3, inner_width)
        .astype(jnp.bfloat16)
    )
    grad_bias_query = jnp.sum(grad_qkv[:, 0].astype(jnp.float32), axis=0)
    grad_bias_value = jnp.sum(grad_qkv[:, 2].astype(jnp.float32), axis=0)
    grad_w_qkv = jnp.einsum("td,tce->dce", tokens, grad_qkv, preferred_element_type=jnp.float32)
    grad_tokens = grad_mid + lax.psum(
        jnp.einsum("tce,dce->td", grad_qkv, full_qkv, preferred_element_type=jnp.float32).astype(
            jnp.bfloat16
        ),
        "tensor",
    ).astype(jnp.float32)
    shard_qkv, shard_out, shard_up, shard_down = (
        lax.psum_scatter(
            grad_w_qkv.astype(jnp.bfloat16), ("fsdp", "context"), scatter_dimension=0, tiled=True
        ).astype(jnp.float32),
        lax.psum_scatter(
            grad_w_attn_out.astype(jnp.bfloat16),
            ("fsdp", "context"),
            scatter_dimension=1,
            tiled=True,
        ).astype(jnp.float32),
        lax.psum_scatter(
            grad_w_up.astype(jnp.bfloat16), ("fsdp", "context"), scatter_dimension=0, tiled=True
        ).astype(jnp.float32),
        lax.psum_scatter(
            grad_w_down.astype(jnp.bfloat16), ("fsdp", "context"), scatter_dimension=1, tiled=True
        ).astype(jnp.float32),
    )
    small_sums = lax.psum(
        (
            grad_bias_query,
            grad_bias_value,
            grad_bias_attn_out,
            grad_gain_one,
            grad_shift_one,
            grad_bias_up,
            grad_bias_down,
            grad_gain_two,
            grad_shift_two,
        ),
        ("fsdp", "context"),
    )
    return (
        output,
        grad_tokens,
        shard_qkv,
        small_sums[0],
        small_sums[1],
        shard_out,
        small_sums[2],
        small_sums[3],
        small_sums[4],
        shard_up,
        small_sums[5],
        shard_down,
        small_sums[6],
        small_sums[7],
        small_sums[8],
    )


MESH = pl.DeviceIdType.MESH
CHUNK = 512
STRETCH = 1024
VMEM_LIMIT = 48 * 1024 * 1024


def ring_place(context, depth):
    z, x = context // 2, context % 2
    return z + x * (2 * depth - 1 - 2 * z)


def ring_context(place, depth):
    x = place // depth
    z = place + x * (2 * depth - 1 - 2 * place)
    return 2 * z + x


def ring_facts(contexts):
    depth = contexts // 2
    fsdp, context = lax.axis_index("fsdp"), lax.axis_index("context")
    place = ring_place(context, depth)

    def at(offset):
        return ring_context((place + offset + 2 * contexts) % contexts, depth)

    return fsdp, context, at


def greet(targets):
    barrier = pltpu.get_barrier_semaphore()
    for target in targets:
        pl.semaphore_signal(barrier, inc=1, device_id=target, device_id_type=MESH)
    pl.semaphore_wait(barrier, len(targets))


def gather_kernel(contexts, count, *refs):
    shards, fulls = refs[:count], refs[count : 2 * count]
    local_sem, send_sem, recv_sem, pair_send, pair_recv = refs[2 * count :]
    fsdp, context, at = ring_facts(contexts)
    half = shards[0].shape[0] // 2
    toward = ({"context": at(1)}, {"context": at(-1)})
    pair = {"fsdp": 1 - fsdp}
    greet([toward[0], toward[1], pair])

    def own(index):
        return pltpu.make_async_copy(
            shards[index], fulls[index].at[fsdp * contexts + context], local_sem.at[index]
        )

    def piece(index, way, step):
        block = fsdp * contexts + at(-step if way == 0 else step)
        return fulls[index].at[block, pl.ds(way * half, half)]

    def hop(index, way, step):
        ref = piece(index, way, step)
        return pltpu.make_async_remote_copy(
            src_ref=ref,
            dst_ref=ref,
            send_sem=send_sem.at[step, index, way],
            recv_sem=recv_sem.at[step, index, way],
            device_id=toward[way],
            device_id_type=MESH,
        )

    def arrival(index, way, step):
        ref = piece(index, way, step + 1)
        return pltpu.make_async_remote_copy(
            src_ref=ref,
            dst_ref=ref,
            send_sem=send_sem.at[step, index, way],
            recv_sem=recv_sem.at[step, index, way],
            device_id=toward[way],
            device_id_type=MESH,
        )

    def across(index, way, step):
        ref = piece(index, way, step)
        return pltpu.make_async_remote_copy(
            src_ref=ref,
            dst_ref=ref,
            send_sem=pair_send.at[step, index, way],
            recv_sem=pair_recv.at[step, index, way],
            device_id=pair,
            device_id_type=MESH,
        )

    def across_arrival(index, way, step):
        block = (1 - fsdp) * contexts + at(-step if way == 0 else step)
        ref = fulls[index].at[block, pl.ds(way * half, half)]
        return pltpu.make_async_remote_copy(
            src_ref=ref,
            dst_ref=ref,
            send_sem=pair_send.at[step, index, way],
            recv_sem=pair_recv.at[step, index, way],
            device_id=pair,
            device_id_type=MESH,
        )

    for index in range(count):
        own(index).start()
    for index in range(count):
        own(index).wait()
        for way in range(2):
            hop(index, way, 0).start()
            across(index, way, 0).start()

    def onward(step, carry):
        for index in range(count):
            for way in range(2):
                arrival(index, way, step - 1).wait_recv()
                hop(index, way, step).start()
                across(index, way, step).start()
        return carry

    lax.fori_loop(1, contexts - 1, onward, 0)
    for index in range(count):
        for way in range(2):
            arrival(index, way, contexts - 2).wait_recv()
            across(index, way, contexts - 1).start()

    def finish(step, carry):
        for index in range(count):
            for way in range(2):
                across(index, way, step).wait_send()
                across_arrival(index, way, step).wait_recv()
        return carry

    def finish_hop(step, carry):
        for index in range(count):
            for way in range(2):
                hop(index, way, step).wait_send()
        return carry

    lax.fori_loop(0, contexts - 1, finish_hop, 0)
    lax.fori_loop(0, contexts, finish, 0)


def gather_rows(shards, contexts, collective_id):
    count = len(shards)
    fulls = pl.pallas_call(
        functools.partial(gather_kernel, contexts, count),
        out_shape=[
            jax.ShapeDtypeStruct((2 * contexts,) + shard.shape, shard.dtype) for shard in shards
        ],
        in_specs=[pl.BlockSpec(memory_space=pl.ANY)] * count,
        out_specs=[pl.BlockSpec(memory_space=pl.ANY)] * count,
        scratch_shapes=[
            pltpu.SemaphoreType.DMA((count,)),
            pltpu.SemaphoreType.DMA((contexts - 1, count, 2)),
            pltpu.SemaphoreType.DMA((contexts - 1, count, 2)),
            pltpu.SemaphoreType.DMA((contexts, count, 2)),
            pltpu.SemaphoreType.DMA((contexts, count, 2)),
        ],
        compiler_params=pltpu.CompilerParams(collective_id=collective_id, has_side_effects=True),
        cost_estimate=pl.CostEstimate(
            flops=0, bytes_accessed=sum(200 * 1024 * shard.shape[1] for shard in shards),
            transcendentals=0,
        ),
        name="gather_rows",
    )(*shards)
    return [full.reshape(-1, full.shape[-1]) for full in fulls]


def scatter_kernel(contexts, count, *refs):
    grads, small = refs[:count], refs[count]
    outs, small_out = refs[count + 1 : 2 * count + 1], refs[2 * count + 1]
    rest = refs[2 * count + 2 :]
    pairs, slots, small_in = rest[:count], rest[count : 2 * count], rest[2 * count]
    small_now = rest[2 * count + 1]
    send_sem, recv_sem, pair_send, pair_recv, small_send, small_recv = rest[2 * count + 2 :]
    fsdp, context, at = ring_facts(contexts)
    half = outs[0].shape[0] // 2
    toward = ({"context": at(1)}, {"context": at(-1)})
    pair = {"fsdp": 1 - fsdp}
    steps = []
    width = 1
    while width < contexts:
        steps.append({"context": context + width - 2 * width * ((context // width) % 2)})
        width *= 2
    partners = [pair] + steps
    greet([toward[0], toward[1]] + partners)

    def rows(way):
        return pl.ds(way * half, half)

    def block_at(way, step):
        return at(-1 - step if way == 0 else 1 + step)

    def across(index, way, step):
        block = block_at(way, step)
        return pltpu.make_async_remote_copy(
            src_ref=grads[index].at[1 - fsdp, block, rows(way)],
            dst_ref=pairs[index].at[block, rows(way)],
            send_sem=pair_send.at[step, index, way],
            recv_sem=pair_recv.at[step, index, way],
            device_id=pair,
            device_id_type=MESH,
        )

    def hop(index, way, step):
        return pltpu.make_async_remote_copy(
            src_ref=pairs[index].at[block_at(way, step), rows(way)],
            dst_ref=slots[index].at[step, rows(way)],
            send_sem=send_sem.at[step, index, way],
            recv_sem=recv_sem.at[step, index, way],
            device_id=toward[way],
            device_id_type=MESH,
        )

    def small_hop(step):
        return pltpu.make_async_remote_copy(
            src_ref=small_now.at[step],
            dst_ref=small_in.at[step],
            send_sem=small_send.at[step],
            recv_sem=small_recv.at[step],
            device_id=partners[step],
            device_id_type=MESH,
        )

    def pair_sum(index, way, step):
        across(index, way, step).wait_recv()
        block = block_at(way, step)
        return grads[index][fsdp, block, rows(way)].astype(jnp.float32) + pairs[index][
            block, rows(way)
        ].astype(jnp.float32)

    small_now[0] = small[...]
    small_hop(0).start()

    def offer(step, carry):
        for index in range(count):
            for way in range(2):
                across(index, way, step).start()
        return carry

    lax.fori_loop(0, contexts, offer, 0)

    for index in range(count):
        for way in range(2):
            total = pair_sum(index, way, 0)
            pairs[index][block_at(way, 0), rows(way)] = total.astype(jnp.bfloat16)
            hop(index, way, 0).start()

    for step in range(len(partners)):
        small_hop(step).wait()
        total = small_now[step] + small_in[step]
        if step + 1 < len(partners):
            small_now[step + 1] = total
            small_hop(step + 1).start()
        else:
            small_out[...] = total

    def onward(step, carry):
        for index in range(count):
            for way in range(2):
                total = pair_sum(index, way, step)
                hop(index, way, step - 1).wait_recv()
                total = total + slots[index][step - 1, rows(way)].astype(jnp.float32)
                pairs[index][block_at(way, step), rows(way)] = total.astype(jnp.bfloat16)
                hop(index, way, step).start()
        return carry

    lax.fori_loop(1, contexts - 1, onward, 0)
    for index in range(count):
        for way in range(2):
            total = pair_sum(index, way, contexts - 1)
            hop(index, way, contexts - 2).wait_recv()
            outs[index][rows(way)] = total + slots[index][contexts - 2, rows(way)].astype(
                jnp.float32
            )

    def finish(step, carry):
        for index in range(count):
            for way in range(2):
                across(index, way, step).wait_send()
        return carry

    def finish_hop(step, carry):
        for index in range(count):
            for way in range(2):
                hop(index, way, step).wait_send()
        return carry

    lax.fori_loop(0, contexts, finish, 0)
    lax.fori_loop(0, contexts - 1, finish_hop, 0)


def scatter_rows(grads, small, contexts, collective_id):
    count = len(grads)
    rows = grads[0].shape[0] // (2 * contexts)
    widths = [grad.shape[1] for grad in grads]
    doubling = 1 + (contexts - 1).bit_length()
    vmem = pl.BlockSpec(memory_space=pltpu.VMEM)
    return pl.pallas_call(
        functools.partial(scatter_kernel, contexts, count),
        out_shape=[jax.ShapeDtypeStruct((rows, width), jnp.float32) for width in widths]
        + [jax.ShapeDtypeStruct(small.shape, jnp.float32)],
        in_specs=[vmem] * (count + 1),
        out_specs=[vmem] * (count + 1),
        scratch_shapes=[pltpu.VMEM((contexts, rows, width), jnp.bfloat16) for width in widths]
        + [pltpu.VMEM((contexts - 1, rows, width), jnp.bfloat16) for width in widths]
        + [
            pltpu.VMEM((doubling,) + small.shape, jnp.float32),
            pltpu.VMEM((doubling,) + small.shape, jnp.float32),
            pltpu.SemaphoreType.DMA((contexts - 1, count, 2)),
            pltpu.SemaphoreType.DMA((contexts - 1, count, 2)),
            pltpu.SemaphoreType.DMA((contexts, count, 2)),
            pltpu.SemaphoreType.DMA((contexts, count, 2)),
            pltpu.SemaphoreType.DMA((doubling,)),
            pltpu.SemaphoreType.DMA((doubling,)),
        ],
        compiler_params=pltpu.CompilerParams(
            collective_id=collective_id, has_side_effects=True, vmem_limit_bytes=VMEM_LIMIT
        ),
        name="scatter_rows",
    )(*[grad.reshape(2, contexts, rows, grad.shape[1]) for grad in grads], small)


def swap_kernel(contexts, to_heads, source, result, local_sem, send_sem, recv_sem):
    context = lax.axis_index("context")
    others = [(context + shift) % contexts for shift in range(1, contexts)]
    greet([{"context": other} for other in others])

    def ends(there):
        if to_heads:
            return source.at[there], result.at[:, context]
        return source.at[:, there], result.at[context]

    here, mine = ends(context)
    keep = pltpu.make_async_copy(here, mine, local_sem)
    copies = []
    for index, other in enumerate(others):
        sent, landed = ends(other)
        copies.append(
            pltpu.make_async_remote_copy(
                src_ref=sent,
                dst_ref=landed,
                send_sem=send_sem.at[index],
                recv_sem=recv_sem.at[index],
                device_id={"context": other},
                device_id_type=MESH,
            )
        )
    for copy in copies:
        copy.start()
    keep.start()
    keep.wait()
    for copy in copies:
        copy.wait()


def swap(source, contexts, to_heads, collective_id):
    shape = (source.shape[1], source.shape[0]) + source.shape[2:]
    return pl.pallas_call(
        functools.partial(swap_kernel, contexts, to_heads),
        out_shape=jax.ShapeDtypeStruct(shape, source.dtype),
        in_specs=[pl.BlockSpec(memory_space=pl.ANY)],
        out_specs=pl.BlockSpec(memory_space=pl.ANY),
        scratch_shapes=[
            pltpu.SemaphoreType.DMA(()),
            pltpu.SemaphoreType.DMA((contexts - 1,)),
            pltpu.SemaphoreType.DMA((contexts - 1,)),
        ],
        compiler_params=pltpu.CompilerParams(collective_id=collective_id, has_side_effects=True),
        name="swap_heads" if to_heads else "swap_rows",
    )(source)


def turned(block):
    return block.astype(jnp.float32).T.astype(jnp.bfloat16)


def key_mask(scores, first_key, low, high):
    keys = first_key + lax.broadcasted_iota(jnp.int32, scores.shape, 0)
    return jnp.where((keys >= low) & (keys < high), scores, MASKED)


def attend_kernel(meta, qkv, att, att_wide, log_total, keys, values, held):
    blocks = qkv.shape[0]

    def lay(block, carry):
        place = pl.ds(pl.multiple_of(block * BLK, BLK), BLK)
        keys[place, :] = turned(qkv[block, HEAD : 2 * HEAD])
        values[:, place] = qkv[block, 2 * HEAD : 3 * HEAD]
        return carry

    lax.fori_loop(0, blocks, lay, 0)

    def one(block, carry):
        begin, low, high = meta[0, block], meta[1, block], meta[2, block]
        query = qkv[block, 0:HEAD]

        def score(stretch, top):
            for part in range(0, STRETCH, CHUNK):
                offset = pl.multiple_of(stretch * STRETCH + part, CHUNK)
                place = pl.ds(pl.multiple_of(begin + offset, BLK), CHUNK)
                scores = jnp.dot(keys[place, :], query, preferred_element_type=jnp.float32)
                scores = key_mask(scores, begin + offset, low, high)
                held[pl.ds(offset, CHUNK)] = scores
                top = jnp.maximum(top, jnp.max(scores, axis=0, keepdims=True))
            return top

        def weigh(stretch, sums):
            total, out = sums
            for part in range(0, STRETCH, CHUNK):
                offset = pl.multiple_of(stretch * STRETCH + part, CHUNK)
                place = pl.ds(pl.multiple_of(begin + offset, BLK), CHUNK)
                prob = jnp.exp(held[pl.ds(offset, CHUNK)] - top)
                total = total + jnp.sum(prob, axis=0, keepdims=True)
                out = out + jnp.dot(
                    values[:, place], prob.astype(jnp.bfloat16), preferred_element_type=jnp.float32
                )
            return total, out

        count = meta[3, block]
        top = lax.fori_loop(0, count, score, jnp.full((1, BLK), MASKED, jnp.float32))
        total, out = lax.fori_loop(
            0,
            count,
            weigh,
            (jnp.zeros((1, BLK), jnp.float32), jnp.zeros((HEAD, BLK), jnp.float32)),
        )
        out = out / total
        att_wide[block] = out
        att[block] = out.astype(jnp.bfloat16)
        log_total[block] = top + jnp.log(total)
        return carry

    lax.fori_loop(0, blocks, one, 0)


def attend(meta, qkv):
    blocks = qkv.shape[0]
    rows = blocks * BLK
    vmem = pl.BlockSpec(memory_space=pltpu.VMEM)
    return pl.pallas_call(
        attend_kernel,
        out_shape=[
            jax.ShapeDtypeStruct((blocks, HEAD, BLK), jnp.bfloat16),
            jax.ShapeDtypeStruct((blocks, HEAD, BLK), jnp.float32),
            jax.ShapeDtypeStruct((blocks, 1, BLK), jnp.float32),
        ],
        in_specs=[pl.BlockSpec(memory_space=pltpu.SMEM), vmem],
        out_specs=[vmem] * 3,
        scratch_shapes=[
            pltpu.VMEM((rows, HEAD), jnp.bfloat16),
            pltpu.VMEM((HEAD, rows), jnp.bfloat16),
            pltpu.VMEM((MAXB * BLK, BLK), jnp.float32),
        ],
        compiler_params=pltpu.CompilerParams(vmem_limit_bytes=VMEM_LIMIT),
        name="attend",
    )(meta, qkv)


def attend_back_kernel(
    meta, qkv, grad_att, att_wide, log_total, grads, keys, keys_turned, values, grad_k, grad_v
):
    blocks = qkv.shape[0]

    def lay(block, carry):
        place = pl.ds(pl.multiple_of(block * BLK, BLK), BLK)
        keys[place, :] = turned(qkv[block, HEAD : 2 * HEAD])
        keys_turned[:, place] = qkv[block, HEAD : 2 * HEAD]
        values[place, :] = turned(qkv[block, 2 * HEAD : 3 * HEAD])
        grad_k[place, :] = jnp.zeros((BLK, HEAD), jnp.float32)
        grad_v[place, :] = jnp.zeros((BLK, HEAD), jnp.float32)
        return carry

    lax.fori_loop(0, blocks, lay, 0)

    def one(block, carry):
        begin, low, high = meta[0, block], meta[1, block], meta[2, block]
        query = qkv[block, 0:HEAD]
        grad = grad_att[block]
        query_rows = turned(query)
        grad_rows = turned(grad)
        delta = jnp.sum(grad.astype(jnp.float32) * att_wide[block], axis=0, keepdims=True)
        log_row = log_total[block]

        def pairs(stretch, grad_q):
            for part in range(0, STRETCH, CHUNK):
                first_key = pl.multiple_of(begin + stretch * STRETCH + part, BLK)
                place = pl.ds(first_key, CHUNK)
                scores = jnp.dot(keys[place, :], query, preferred_element_type=jnp.float32)
                prob = jnp.exp(key_mask(scores, first_key, low, high) - log_row)
                grad_prob = jnp.dot(values[place, :], grad, preferred_element_type=jnp.float32)
                grad_score = (prob * (grad_prob - delta)).astype(jnp.bfloat16)
                grad_q = grad_q + jnp.dot(
                    keys_turned[:, place], grad_score, preferred_element_type=jnp.float32
                )
                grad_k[place, :] += jnp.dot(
                    grad_score, query_rows, preferred_element_type=jnp.float32
                )
                grad_v[place, :] += jnp.dot(
                    prob.astype(jnp.bfloat16), grad_rows, preferred_element_type=jnp.float32
                )
            return grad_q

        grad_q = lax.fori_loop(
            0, meta[3, block], pairs, jnp.zeros((HEAD, BLK), jnp.float32)
        )
        grads[block, 0:HEAD] = (grad_q * HEAD ** (-0.5)).astype(jnp.bfloat16)
        return carry

    lax.fori_loop(0, blocks, one, 0)

    def store(block, carry):
        place = pl.ds(pl.multiple_of(block * BLK, BLK), BLK)
        grads[block, HEAD : 2 * HEAD] = grad_k[place, :].T.astype(jnp.bfloat16)
        grads[block, 2 * HEAD : 3 * HEAD] = grad_v[place, :].T.astype(jnp.bfloat16)
        return carry

    lax.fori_loop(0, blocks, store, 0)


def attend_back(meta, qkv, grad_att, att_wide, log_total):
    blocks = qkv.shape[0]
    rows = blocks * BLK
    vmem = pl.BlockSpec(memory_space=pltpu.VMEM)
    return pl.pallas_call(
        attend_back_kernel,
        out_shape=jax.ShapeDtypeStruct(qkv.shape, jnp.bfloat16),
        in_specs=[pl.BlockSpec(memory_space=pltpu.SMEM)] + [vmem] * 4,
        out_specs=vmem,
        scratch_shapes=[
            pltpu.VMEM((rows, HEAD), jnp.bfloat16),
            pltpu.VMEM((HEAD, rows), jnp.bfloat16),
            pltpu.VMEM((rows, HEAD), jnp.bfloat16),
            pltpu.VMEM((rows, HEAD), jnp.float32),
            pltpu.VMEM((rows, HEAD), jnp.float32),
        ],
        compiler_params=pltpu.CompilerParams(vmem_limit_bytes=VMEM_LIMIT),
        name="attend_back",
    )(meta, qkv, grad_att, att_wide, log_total)


def over_tensor(low):
    other = lax.ppermute(low, "tensor", [(0, 1), (1, 0)])
    return low.astype(jnp.float32) + other.astype(jnp.float32)


def ring_device(
    tokens,
    doc_blocks,
    pad_tokens,
    w_qkv,
    bias_query,
    bias_value,
    w_attn_out,
    bias_attn_out,
    gain_one,
    shift_one,
    w_up,
    bias_up,
    w_down,
    bias_down,
    gain_two,
    shift_two,
    cotangent,
):
    contexts = lax.axis_size("context")
    row_count, width = tokens.shape
    slots = row_count // BLK
    inner_width = w_qkv.shape[2]
    heads_here = inner_width // HEAD
    blocks = slots * contexts
    wide = functools.partial(jnp.einsum, preferred_element_type=jnp.float32)

    doc_ends = jnp.cumsum(doc_blocks[0]) * BLK
    firsts = jnp.arange(blocks, dtype=jnp.int32) * BLK
    doc_of_block = jnp.sum((firsts[:, None] >= doc_ends[None, :]).astype(jnp.int32), axis=1)
    chosen = doc_of_block[:, None] == jnp.arange(doc_ends.shape[0], dtype=jnp.int32)[None, :]
    low = jnp.sum(jnp.where(chosen, doc_ends - doc_blocks[0] * BLK, 0), axis=1)
    high = jnp.sum(jnp.where(chosen, doc_ends - pad_tokens[0], 0), axis=1)
    stretches = (high - low + STRETCH - 1) // STRETCH
    begin = jnp.minimum(low, blocks * BLK - stretches * STRETCH)
    meta = jnp.stack([begin, low, high, stretches]).astype(jnp.int32)

    full_qkv, full_out = gather_rows(
        [w_qkv.reshape(w_qkv.shape[0], -1), w_attn_out.T], contexts, 0
    )

    bias_three = jnp.concatenate([bias_query, jnp.zeros_like(bias_query), bias_value])
    qkv = (wide("td,df->tf", tokens, full_qkv) + bias_three).astype(jnp.bfloat16)
    query_scale = jnp.concatenate(
        [jnp.full((inner_width,), HEAD ** (-0.5)), jnp.ones((2 * inner_width,))]
    ).astype(jnp.bfloat16)
    qkv_heads = (
        (qkv * query_scale)
        .reshape(slots, BLK, 3, heads_here, HEAD)
        .transpose(3, 0, 2, 4, 1)
        .reshape(heads_here, slots, 3 * HEAD, BLK)
    )
    qkv_here = swap(qkv_heads, contexts, True, 1).reshape(blocks, 3 * HEAD, BLK)
    att_low, att_wide, log_total = attend(meta, qkv_here)
    att_back = swap(att_low.reshape(slots, contexts, HEAD, BLK), contexts, False, 2)
    attended_low = att_back.transpose(1, 3, 0, 2).reshape(row_count, inner_width)

    branch_part = wide("te,de->td", attended_low, full_out).astype(jnp.bfloat16)
    branch_part, shard_up, shard_down = lax.optimization_barrier((branch_part, w_up, w_down.T))
    branch = over_tensor(branch_part) + bias_attn_out
    full_up, full_down = gather_rows([shard_up, shard_down], contexts, 6)
    first, normed_one, factor_one = layer_norm(
        tokens.astype(jnp.float32) + branch, gain_one, shift_one
    )
    first_low = first.astype(jnp.bfloat16)
    acts, gelu_backs, feeds = [], [], []
    for part in jnp.split(first_low, 2):
        pre = wide("td,df->tf", part, full_up) + bias_up
        act, gelu_back = jax.vjp(lambda hidden: jax.nn.gelu(hidden, approximate=False), pre)
        acts.append(act.astype(jnp.bfloat16))
        gelu_backs.append(gelu_back)
        feeds.append(over_tensor(wide("tf,df->td", acts[-1], full_down).astype(jnp.bfloat16)))
    act_low = jnp.concatenate(acts)
    feed = jnp.concatenate(feeds) + bias_down
    out, normed_two, factor_two = layer_norm(first + feed, gain_two, shift_two)
    output = out.astype(jnp.bfloat16)

    grad_out = cotangent.astype(jnp.float32)
    grad_gain_two = jnp.sum(grad_out * normed_two, axis=0)
    grad_shift_two = jnp.sum(grad_out, axis=0)
    grad_second = norm_back(grad_out, normed_two, factor_two, gain_two)
    grad_feed = grad_second.astype(jnp.bfloat16)
    grad_bias_down = jnp.sum(grad_feed.astype(jnp.float32), axis=0)
    grad_pres, grad_firsts = [], []
    for part, gelu_back in zip(jnp.split(grad_feed, 2), gelu_backs):
        grad_act = wide("td,df->tf", part, full_down)
        grad_pres.append(gelu_back(grad_act)[0].astype(jnp.bfloat16))
        grad_firsts.append(
            over_tensor(wide("tf,df->td", grad_pres[-1], full_up).astype(jnp.bfloat16))
        )
    grad_pre = jnp.concatenate(grad_pres)
    grad_bias_up = jnp.sum(grad_pre.astype(jnp.float32), axis=0)
    grad_first = grad_second + jnp.concatenate(grad_firsts)
    grad_w_down = wide("td,tf->df", grad_feed, act_low).astype(jnp.bfloat16)
    grad_w_up = wide("td,tf->df", first_low, grad_pre).astype(jnp.bfloat16)
    grad_gain_one = jnp.sum(grad_first * normed_one, axis=0)
    grad_shift_one = jnp.sum(grad_first, axis=0)
    grad_mid = norm_back(grad_first, normed_one, factor_one, gain_one)
    grad_branch = grad_mid.astype(jnp.bfloat16)
    grad_bias_attn_out = jnp.sum(grad_branch.astype(jnp.float32), axis=0)
    grad_w_attn_out = wide("td,te->de", grad_branch, attended_low).astype(jnp.bfloat16)
    grad_att = (
        wide("td,de->te", grad_branch, full_out)
        .astype(jnp.bfloat16)
        .reshape(slots, BLK, heads_here, HEAD)
        .transpose(2, 0, 3, 1)
    )
    grad_att_here = swap(grad_att, contexts, True, 3).reshape(blocks, HEAD, BLK)
    grad_here = attend_back(meta, qkv_here, grad_att_here, att_wide, log_total)
    grad_qkv = (
        swap(grad_here.reshape(slots, contexts, 3 * HEAD, BLK), contexts, False, 4)
        .reshape(heads_here, slots, 3, HEAD, BLK)
        .transpose(1, 4, 2, 0, 3)
        .reshape(row_count, 3 * inner_width)
    )
    grad_bias = jnp.sum(grad_qkv.astype(jnp.float32), axis=0)
    grad_tokens = grad_mid + over_tensor(
        wide("tf,df->td", grad_qkv, full_qkv).astype(jnp.bfloat16)
    )
    grad_w_qkv = wide("td,tf->df", tokens, grad_qkv).astype(jnp.bfloat16)
    smalls = [
        grad_bias[:inner_width],
        grad_bias[2 * inner_width :],
        grad_bias_attn_out,
        grad_gain_one,
        grad_shift_one,
        grad_bias_up,
        grad_bias_down,
        grad_gain_two,
        grad_shift_two,
    ]
    shard_qkv, shard_out, shard_up, shard_down, small_rows = scatter_rows(
        [grad_w_qkv, grad_w_attn_out, grad_w_up, grad_w_down],
        jnp.concatenate(smalls).reshape(-1, 128),
        contexts,
        5,
    )
    flat = small_rows.reshape(-1)
    sums = []
    start = 0
    for small in smalls:
        sums.append(flat[start : start + small.shape[0]])
        start += small.shape[0]
    return (
        output,
        grad_tokens,
        shard_qkv.reshape(w_qkv.shape),
        sums[0],
        sums[1],
        shard_out.T,
        sums[2],
        sums[3],
        sums[4],
        shard_up,
        sums[5],
        shard_down.T,
        sums[6],
        sums[7],
        sums[8],
    )


def solution(mesh):
    in_specs = (
        P(("fsdp", "context"), None),
        P("fsdp", None),
        P("fsdp", None),
        P(("fsdp", "context"), None, "tensor"),
        P("tensor"),
        P("tensor"),
        P("tensor", ("fsdp", "context")),
        P(),
        P(),
        P(),
        P(("fsdp", "context"), "tensor"),
        P("tensor"),
        P("tensor", ("fsdp", "context")),
        P(),
        P(),
        P(),
        P(("fsdp", "context"), None),
    )
    out_specs = (
        P(("fsdp", "context"), None),
        P(("fsdp", "context"), None),
        P(("fsdp", "context"), None, "tensor"),
        P("tensor"),
        P("tensor"),
        P("tensor", ("fsdp", "context")),
        P(),
        P(),
        P(),
        P(("fsdp", "context"), "tensor"),
        P("tensor"),
        P("tensor", ("fsdp", "context")),
        P(),
        P(),
        P(),
    )
    contexts = mesh.shape["context"]
    heads_each = 1024 // HEAD // mesh.shape["tensor"]
    fits = (
        mesh.shape["fsdp"] == 2
        and mesh.shape["tensor"] == 2
        and contexts == 8
        and heads_each == contexts
    )
    return jax.shard_map(
        ring_device if fits else per_device, mesh=mesh, in_specs=in_specs, out_specs=out_specs, check_vma=False
    )
```
